32 devices in a mesh: gx: 8 (over y, x, core), gy: 4 (over z).
Axes of the slice: x: 2, y: 2, z: 4, core: 2. Of those that a mesh axis runs over, the one named last changes fastest.
Arguments:
- momenta: float32 [3, 16, 32, 1024], P(None, None, 'gy', 'gx'), may hold values from -6 to 6
- theta: float32 [16, 32, 1024], P(None, 'gy', 'gx'), may hold values from -6 to 6
- courant: float32 [3, 16, 32, 1024], P(None, None, 'gy', 'gx'), may hold values from -0.3 to 0.3
- density: float32 [16, 32, 1024], P(None, 'gy', 'gx'), may hold values from 0.8 to 1.6
- metric_diag: float32 [3, 16, 32, 1024], P(None, None, 'gy', 'gx'), may hold values from 0.5 to 2
- metric_cross: float32 [3, 16, 32, 1024], P(None, None, 'gy', 'gx'), may hold values from -0.2 to 0.2
Outputs:
- momenta_out: float32 [3, 16, 32, 1024], P(None, None, 'gy', 'gx')
- theta_out: float32 [16, 32, 1024], P(None, 'gy', 'gx')
- pressure: float32 [16, 32, 1024], P(None, 'gy', 'gx')
The draws below stay inside these ranges and needn't reach their ends.
All inputs are finite; a program needn't handle non-finite values.
Results may differ from the reference program's by a relative error of at most 0.0003.
Values sent between devices are 32-bit elements; how exact they have to be, the bound alone decides.
A program may use at most 64 MiB of HBM per device.

```python
import math
import jax
import jax.numpy as jnp

NZ = 16
ITERS = 3
NX = 1024
NY = 32


def steps_of(key, shape, pieces, low, top_value):
    def one(axis_at, shards_of):
        draws = jax.random.uniform(jax.random.fold_in(jax.random.fold_in(key, 6), axis_at), (shards_of,), jnp.float32, low / len(pieces), top_value / len(pieces))
        return jnp.repeat(jnp.exp(draws), shape[axis_at] // shards_of).reshape((-1,) + (1,) * (len(shape) - axis_at - 1))

    factor_of = one(*pieces[0])
    for cut in pieces[1:]:
        factor_of = factor_of * one(*cut)
    return factor_of


def centred(stream_key, dims, width, bound, cuts=(), held_as=jnp.bfloat16):
    values = jax.random.normal(stream_key, dims, jnp.float32) * width
    if len(cuts) > 0:
        values = steps_of(stream_key, dims, cuts, -0.22, 0.18) * values
    return jnp.clip(values, min=-bound, max=bound).astype(held_as)


def setup_inputs(seed: int = 0) -> dict:
    key_of = jax.random.split(jax.random.key(seed), 7)
    momenta = centred(key_of[0], (3, NZ, NY, NX), 1.0, 6.0, ((2, 4), (3, 8)), jnp.float32)
    theta = centred(key_of[1], (NZ, NY, NX), 1.0, 6.0, ((1, 4), (2, 8)), jnp.float32)
    courant = jnp.clip(jax.random.uniform(key_of[2], (3, NZ, NY, NX), jnp.float32, -0.3, 0.3) * steps_of(key_of[2], (3, NZ, NY, NX), ((2, 4), (3, 8)), -0.4, 0.0), -0.3, 0.3)
    density = jnp.clip(0.8 + 0.8 * jax.random.uniform(key_of[3], (NZ, NY, NX), jnp.float32) ** steps_of(key_of[3], (NZ, NY, NX), ((1, 4), (2, 8)), -0.2, 0.2), 0.8, 1.6)
    metric_diag = jnp.clip(jnp.exp(math.log(2.0) - 1.3862944 * jax.random.uniform(key_of[4], (3, NZ, NY, NX), jnp.float32) ** steps_of(key_of[4], (3, NZ, NY, NX), ((2, 4), (3, 8)), -0.2, 0.2)), 0.5, 2.0)
    metric_cross = jnp.clip(jax.random.uniform(key_of[5], (3, NZ, NY, NX), jnp.float32, -0.2, 0.2) * steps_of(key_of[5], (3, NZ, NY, NX), ((2, 4), (3, 8)), -0.4, 0.0), -0.2, 0.2)
    return {"momenta": momenta, "theta": theta, "courant": courant, "density": density, "metric_diag": metric_diag, "metric_cross": metric_cross}


helm = 0.02


def zshift(a, dz):
    if dz == 0:
        return a
    if dz > 0:
        return jnp.concatenate((a[..., dz:, :, :], jnp.zeros_like(a[..., :dz, :, :])), axis=-3)
    return jnp.concatenate((jnp.zeros_like(a[..., dz:, :, :]), a[..., :dz, :, :]), axis=-3)


def yshift(a, dy):
    if dy == 0:
        return a
    if dy > 0:
        return jnp.concatenate((a[..., dy:, :], jnp.zeros_like(a[..., :dy, :])), axis=-2)
    return jnp.concatenate((jnp.zeros_like(a[..., dy:, :]), a[..., :dy, :]), axis=-2)


def shifted(a, dz, dy, dx):
    if dx != 0:
        a = jnp.roll(a, -dx, axis=-1)
    return zshift(yshift(a, dy), dz)


def donor(left, right, courant):
    return jnp.maximum(courant, 0.0) * left + jnp.minimum(courant, 0.0) * right


def antidiff(left, right, courant, dens_left, dens_right):
    return 0.5 * (jnp.abs(courant) - courant * courant / (0.5 * (dens_left + dens_right))) * (right - left)


def upwind_pass(look, field, dens, cx, cy, cz):
    centre = look(field, 0, 0, 0)
    fxr = donor(centre, look(field, 0, 0, 1), look(cx, 0, 0, 1))
    fxl = donor(look(field, 0, 0, -1), centre, look(cx, 0, 0, 0))
    fyr = donor(centre, look(field, 0, 1, 0), look(cy, 0, 1, 0))
    fyl = donor(look(field, 0, -1, 0), centre, look(cy, 0, 0, 0))
    fzr = donor(centre, look(field, 1, 0, 0), look(cz, 1, 0, 0))
    fzl = donor(look(field, -1, 0, 0), centre, look(cz, 0, 0, 0))
    return centre - (fxr - fxl + fyr - fyl + fzr - fzl) / look(dens, 0, 0, 0)


def anti_pass(look_new, look_old, first, dens, cx, cy, cz):
    centre = look_new(first, 0, 0, 0)
    here = look_old(dens, 0, 0, 0)
    axr = antidiff(centre, look_new(first, 0, 0, 1), look_old(cx, 0, 0, 1), here, look_old(dens, 0, 0, 1))
    axl = antidiff(look_new(first, 0, 0, -1), centre, look_old(cx, 0, 0, 0), look_old(dens, 0, 0, -1), here)
    ayr = antidiff(centre, look_new(first, 0, 1, 0), look_old(cy, 0, 1, 0), here, look_old(dens, 0, 1, 0))
    ayl = antidiff(look_new(first, 0, -1, 0), centre, look_old(cy, 0, 0, 0), look_old(dens, 0, -1, 0), here)
    azr = antidiff(centre, look_new(first, 1, 0, 0), look_old(cz, 1, 0, 0), here, look_old(dens, 1, 0, 0))
    azl = antidiff(look_new(first, -1, 0, 0), centre, look_old(cz, 0, 0, 0), look_old(dens, -1, 0, 0), here)
    return centre - (axr - axl + ayr - ayl + azr - azl) / here


def coefficients(look, a_one, a_two, a_three, cross, upper_y, lower_y, upper_z, lower_z):
    wx = 0.5 * (look(a_one, 0, 0, 0) + look(a_one, 0, 0, 1))
    wxl = 0.5 * (look(a_one, 0, 0, -1) + look(a_one, 0, 0, 0))
    wy = 0.5 * (look(a_two, 0, 0, 0) + look(a_two, 0, 1, 0)) * upper_y
    wyl = 0.5 * (look(a_two, 0, -1, 0) + look(a_two, 0, 0, 0)) * lower_y
    wz = 0.5 * (a_three + zshift(a_three, 1)) * upper_z
    wzl = 0.5 * (zshift(a_three, -1) + a_three) * lower_z
    return (wx, wxl, wy, wyl, wz, wzl, cross[0], cross[1], cross[2])


def operate(look, field, coef):
    wx, wxl, wy, wyl, wz, wzl, c_xy, c_xz, c_yz = coef
    centre = look(field, 0, 0, 0)
    flow_x = wx * (look(field, 0, 0, 1) - centre) - wxl * (centre - look(field, 0, 0, -1))
    flow_y = wy * (look(field, 0, 1, 0) - centre) - wyl * (centre - look(field, 0, -1, 0))
    flow_z = wz * (look(field, 1, 0, 0) - centre) - wzl * (centre - look(field, -1, 0, 0))
    d_xy = 0.25 * ((look(field, 0, 1, 1) - look(field, 0, 1, -1)) - (look(field, 0, -1, 1) - look(field, 0, -1, -1)))
    d_xz = 0.25 * ((look(field, 1, 0, 1) - look(field, 1, 0, -1)) - (look(field, -1, 0, 1) - look(field, -1, 0, -1)))
    d_yz = 0.25 * ((look(field, 1, 1, 0) - look(field, 1, -1, 0)) - (look(field, -1, 1, 0) - look(field, -1, -1, 0)))
    return flow_x + flow_y + flow_z + c_xy * d_xy + c_xz * d_xz + c_yz * d_yz - helm * centre


def reference(momenta, theta, courant, density, metric_diag, metric_cross):
    rows = jnp.arange(NY, dtype=jnp.int32)[:, None]
    levels = jnp.arange(NZ, dtype=jnp.int32)[:, None, None]
    cx = courant[0]
    cy = courant[1] * (rows != 0).astype(jnp.float32)
    cz = courant[2] * (levels != 0).astype(jnp.float32)
    fields = [momenta[0], momenta[1], momenta[2], theta]
    moved = []
    for field in fields:
        first = upwind_pass(shifted, field, density, cx, cy, cz)
        moved.append(anti_pass(shifted, shifted, first, density, cx, cy, cz))
    uflow, vflow, wflow, theta_out = moved
    rhs = 0.5 * (shifted(uflow, 0, 0, 1) - shifted(uflow, 0, 0, -1)) + 0.5 * (shifted(vflow, 0, 1, 0) - shifted(vflow, 0, -1, 0)) + 0.5 * (zshift(wflow, 1) - zshift(wflow, -1))
    upper_y = (rows < NY - 1).astype(jnp.float32)
    lower_y = (rows > 0).astype(jnp.float32)
    upper_z = (levels < NZ - 1).astype(jnp.float32)
    lower_z = (levels > 0).astype(jnp.float32)
    coef = coefficients(shifted, metric_diag[0], metric_diag[1], metric_diag[2], metric_cross, upper_y, lower_y, upper_z, lower_z)
    solution = jnp.zeros_like(rhs)
    resid = rhs
    dirs = [resid]
    images = [operate(shifted, resid, coef)]
    norms = [jnp.sum(images[0] * images[0])]
    for step in range(ITERS):
        beta = jnp.sum(resid * images[step]) / norms[step]
        solution = solution + beta * dirs[step]
        resid = resid - beta * images[step]
        if step + 1 < ITERS:
            lifted = operate(shifted, resid, coef)
            new_dir = resid
            new_img = lifted
            for back in range(step + 1):
                alpha = jnp.sum(lifted * images[back]) / norms[back]
                new_dir = new_dir - alpha * dirs[back]
                new_img = new_img - alpha * images[back]
            dirs.append(new_dir)
            images.append(new_img)
            norms.append(jnp.sum(new_img * new_img))
    grad_x = 0.5 * (shifted(solution, 0, 0, 1) - shifted(solution, 0, 0, -1))
    grad_y = 0.5 * (shifted(solution, 0, 1, 0) - shifted(solution, 0, -1, 0))
    grad_z = 0.5 * (zshift(solution, 1) - zshift(solution, -1))
    momenta_out = jnp.stack((uflow - grad_x, vflow - grad_y, wflow - grad_z), axis=0)
    return momenta_out, theta_out, solution
```

```python
import functools

import jax
import jax.numpy as jnp
from jax import lax
from jax.experimental import pallas as pl
from jax.experimental.pallas import tpu as pltpu
from jax.sharding import PartitionSpec as P

ITERS = 3
HELM = 0.02
SHIFT = 6.0
MESH = pl.DeviceIdType.MESH

ORDER = (1, 5, 7, 0, 2, 4, 6, 9, 8, 10, 11, 12, 13, 3)
V, CY, RHO, U, W, CX, CZ, A22, A11, A33, A12, A13, A23, TH = range(14)
HALF = 7
THIRD = (2, 1)


def kernel(nx, ny, mom, theta, cour, dens, diag, cross, mom_out, th_out, p_out,
           cells, rows, edges, packed, beside, corner, first, second, coef,
           kry, rhs_rows, rhs_edges, rhs_packed, rhs_beside, rhs_corner,
           part, part_x, sum_x, part_y, in_sem, send_sem, recv_sem):
    gx = lax.axis_index("gx")
    gy = lax.axis_index("gy")
    nz = rows.shape[2]
    ny_dev = 8
    plane = nz * ny_dev

    def device(dx, dy):
        return {"gx": lax.rem(gx + dx + nx, nx), "gy": gy + dy}

    barrier = pltpu.get_barrier_semaphore()
    peers = [(lax.rem(gx + d, nx), gy) for d in range(1, nx)]
    peers += [(gx, lax.rem(gy + d, ny)) for d in range(1, ny)]
    peers += [(lax.rem(gx + a, nx), lax.rem(gy + b, ny)) for a in (1, nx - 1) for b in (1, ny - 1)]
    for a, b in peers:
        pl.semaphore_signal(barrier, inc=1, device_id={"gx": a, "gy": b}, device_id_type=MESH)

    loads = []
    place = 0
    for n, ref in enumerate((mom, theta, cour, dens, diag, cross)):
        size = ref.shape[0]
        loads.append(pltpu.make_async_copy(ref, cells.at[pl.ds(place, size)], in_sem.at[n]))
        place += size
    for n in (0, 2, 3, 1, 4, 5):
        loads[n].start()

    def clear(lo):
        rows[lo:lo + 3] = jnp.zeros((3,) + rows.shape[1:], jnp.float32)
        edges[lo:lo + 3] = jnp.zeros((3,) + edges.shape[1:], jnp.float32)
        for i in range(lo, lo + 3):
            rows[i, RHO] = jnp.ones(rows.shape[2:], jnp.float32)
            edges[i, RHO] = jnp.ones(rows.shape[2:], jnp.float32)
        rhs_rows[lo:lo + 3] = jnp.zeros((3,) + rhs_rows.shape[1:], jnp.float32)
        rhs_edges[lo:lo + 3] = jnp.zeros((3,) + rhs_edges.shape[1:], jnp.float32)

    pl.when(gy == 0)(lambda: clear(0))
    pl.when(gy == ny - 1)(lambda: clear(11))

    lane = lax.broadcasted_iota(jnp.int32, (nz, 128), 1)
    level = lax.broadcasted_iota(jnp.int32, (nz, 128), 0)
    slot = lane // 8
    from_left = lax.rem(lane, 8) < 4
    wide_level = lax.broadcasted_iota(jnp.int32, (nz, 256), 0)
    last = wide_level == nz - 1
    ground = wide_level == 0

    def xm(a):
        return pltpu.roll(a, 1, 1)

    def xp(a):
        return pltpu.roll(a, 255, 1)

    def zp(a):
        return jnp.where(last, 0.0, pltpu.roll(a, nz - 1, 0))

    def zm(a):
        return jnp.where(ground, 0.0, pltpu.roll(a, 1, 0))

    def load_half(b):
        def one(j, _):
            for f in range(b * HALF, b * HALF + HALF):
                value = cells[pl.ds(ORDER[f] * plane + j, nz, stride=ny_dev), :]
                if f == CY:
                    value = jnp.where(gy * ny_dev + j == 0, 0.0, value)
                if f == CZ:
                    value = jnp.where(level == 0, 0.0, value)
                rows[3 + j, f] = value
            return 0
        lax.fori_loop(0, ny_dev, one, 0)

    def pack_half(b):
        def one(t, _):
            acc = jnp.zeros((nz, 128), jnp.float32)
            for side in range(2):
                for fi in range(HALF):
                    p = 64 * side + 8 * fi
                    moved = pltpu.roll(rows[3 + 2 * t + side, b * HALF + fi], (p + 4) % 128, 1)
                    acc = jnp.where(slot == p // 8, moved, acc)
            packed[b, t] = acc
            return 0
        lax.fori_loop(0, ny_dev // 2, one, 0)

    def unpack_half(b):
        def spread(tile, side, row, count):
            for fi in range(count):
                p = 64 * side + 8 * fi
                edges[row, b * HALF + fi] = pltpu.roll(tile, (128 - (p + 4)) % 128, 1)

        def one(t, _):
            tile = jnp.where(from_left, beside[b, 0, t], beside[b, 1, t])
            for side in range(2):
                spread(tile, side, 3 + 2 * t + side, HALF)
            return 0
        lax.fori_loop(0, ny_dev // 2, one, 0)

        @pl.when(gy > 0)
        def _():
            for j in (5, 6, 7):
                tile = jnp.where(from_left, corner[b, 0, 0, j // 2 - 2], corner[b, 0, 1, j // 2 - 2])
                spread(tile, j % 2, j - 5, THIRD[b] if j == 5 else HALF)

        @pl.when(gy < ny - 1)
        def _():
            for j in (0, 1, 2):
                tile = jnp.where(from_left, corner[b, 1, 0, j // 2], corner[b, 1, 1, j // 2])
                spread(tile, j % 2, 11 + j, THIRD[b] if j == 2 else HALF)

    def remote(src, dst, k, dx, dy):
        return pltpu.make_async_remote_copy(
            src_ref=src, dst_ref=dst, send_sem=send_sem.at[k], recv_sem=recv_sem.at[k],
            device_id=device(dx, dy), device_id_type=MESH)

    def group(entries, base):
        by = {1: [], -1: [], 0: []}
        for n, (dx, dy, src, dst) in enumerate(entries):
            by[dy].append((src, dst, base + n, dx, dy))
        return by

    def each(by, action, sign):
        for dy in (1, -1, 0):
            def run(dy=dy):
                for item in by[dy]:
                    action(remote(*item))
            if dy == 0:
                run()
            elif dy * sign == 1:
                pl.when(gy < ny - 1)(run)
            else:
                pl.when(gy > 0)(run)

    def start(by):
        each(by, lambda c: c.start(), 1)

    def wait_recv(by):
        each(by, lambda c: c.wait_recv(), -1)

    def wait_send(by):
        each(by, lambda c: c.wait_send(), 1)

    def half_entries(b):
        fs = pl.ds(b * HALF, HALF)
        ft = pl.ds(b * HALF, THIRD[b])
        return [
            (0, 1, rows.at[pl.ds(9, 2), fs], rows.at[pl.ds(1, 2), fs]),
            (0, 1, rows.at[pl.ds(8, 1), ft], rows.at[pl.ds(0, 1), ft]),
            (0, -1, rows.at[pl.ds(3, 2), fs], rows.at[pl.ds(11, 2), fs]),
            (0, -1, rows.at[pl.ds(5, 1), ft], rows.at[pl.ds(13, 1), ft]),
            (1, 0, packed.at[b], beside.at[b, 0]),
            (-1, 0, packed.at[b], beside.at[b, 1]),
            (1, 1, packed.at[b, pl.ds(2, 2)], corner.at[b, 0, 0]),
            (-1, 1, packed.at[b, pl.ds(2, 2)], corner.at[b, 0, 1]),
            (1, -1, packed.at[b, pl.ds(0, 2)], corner.at[b, 1, 0]),
            (-1, -1, packed.at[b, pl.ds(0, 2)], corner.at[b, 1, 1]),
        ]

    half_a = group(half_entries(0), 0)
    half_b = group(half_entries(1), 10)
    half_r = group([
        (0, 1, rhs_rows.at[pl.ds(8, 3)], rhs_rows.at[pl.ds(0, 3)]),
        (0, -1, rhs_rows.at[pl.ds(3, 3)], rhs_rows.at[pl.ds(11, 3)]),
        (1, 0, rhs_packed, rhs_beside.at[0]),
        (-1, 0, rhs_packed, rhs_beside.at[1]),
        (1, 1, rhs_packed, rhs_corner.at[0, 0]),
        (-1, 1, rhs_packed, rhs_corner.at[0, 1]),
        (1, -1, rhs_packed, rhs_corner.at[1, 0]),
        (-1, -1, rhs_packed, rhs_corner.at[1, 1]),
    ], 20)

    for n in (0, 2, 3):
        loads[n].wait()
    load_half(0)
    pack_half(0)
    pl.semaphore_wait(barrier, len(peers))
    start(half_a)
    for n in (1, 4, 5):
        loads[n].wait()
    load_half(1)
    pack_half(1)
    start(half_b)

    def wide(r, f):
        return jnp.concatenate([rows[r, f], edges[r, f]], axis=1)

    def upwind(fields, lo, hi):
        def one(r, _):
            cx, cy, cy_up, cz = wide(r, CX), wide(r, CY), wide(r + 1, CY), wide(r, CZ)
            inv = 1.0 / wide(r, RHO)
            cx_p, cx_n = jnp.maximum(cx, 0.0), jnp.minimum(cx, 0.0)
            cy_p, cy_n = jnp.maximum(cy, 0.0), jnp.minimum(cy, 0.0)
            cu_p, cu_n = jnp.maximum(cy_up, 0.0), jnp.minimum(cy_up, 0.0)
            cz_p, cz_n = jnp.maximum(cz, 0.0), jnp.minimum(cz, 0.0)
            for n, f in fields:
                here = wide(r, f)
                fx = cx_p * xm(here) + cx_n * here
                fz = cz_p * zm(here) + cz_n * here
                fy = cy_p * wide(r - 1, f) + cy_n * here
                fu = cu_p * here + cu_n * wide(r + 1, f)
                total = xp(fx) - fx + fu - fy + zp(fz) - fz
                first[r, n] = here - total * inv
            return 0
        lax.fori_loop(lo, hi, one, 0)

    def antidiffuse(fields, lo, hi):
        def one(r, _):
            cx, cy, cy_up, cz = wide(r, CX), wide(r, CY), wide(r + 1, CY), wide(r, CZ)
            rho = wide(r, RHO)
            inv = 1.0 / rho

            def face(c, a, b):
                return 0.5 * jnp.abs(c) - c * c / (a + b)

            kx = face(cx, xm(rho), rho)
            ky = face(cy, wide(r - 1, RHO), rho)
            ku = face(cy_up, rho, wide(r + 1, RHO))
            kz = face(cz, zm(rho), rho)
            for n in fields:
                here = first[r, n]
                ax = kx * (here - xm(here))
                az = kz * (here - zm(here))
                ay = ky * (here - first[r - 1, n])
                au = ku * (first[r + 1, n] - here)
                total = xp(ax) - ax + au - ay + zp(az) - az
                second[r, n] = here - total * inv
            return 0
        lax.fori_loop(lo, hi, one, 0)

    wait_recv(half_a)
    unpack_half(0)
    upwind(((0, U), (1, V), (2, W)), 1, 13)
    antidiffuse((0, 1, 2), 2, 12)

    def make_rhs(j, acc):
        r = 3 + j
        u, w = second[r, 0], second[r, 2]
        value = (0.5 * (xp(u) - xm(u)) + 0.5 * (second[r + 1, 1] - second[r - 1, 1])
                 + 0.5 * (zp(w) - zm(w)))[:, :128]
        rhs_rows[r] = value
        return jnp.where(slot == j, pltpu.roll(value, 8 * j + 4, 1), acc)

    rhs_packed[...] = lax.fori_loop(0, ny_dev, make_rhs, jnp.zeros((nz, 128), jnp.float32))
    start(half_r)

    wait_recv(half_b)
    unpack_half(1)

    def make_coef(r, _):
        a11, a22, a33 = wide(r, A11), wide(r, A22), wide(r, A33)
        at = gy * ny_dev + r - 3
        wxl = 0.5 * (xm(a11) + a11)
        wx = xp(wxl)
        wyl = jnp.where((at > 0) & (at < ny * ny_dev), 0.5 * (wide(r - 1, A22) + a22), 0.0)
        wy = jnp.where((at > -1) & (at < ny * ny_dev - 1), 0.5 * (a22 + wide(r + 1, A22)), 0.0)
        wzl = jnp.where(ground, 0.0, 0.5 * (zm(a33) + a33))
        wz = zp(wzl)
        coef[r, 0] = wx
        coef[r, 1] = wxl
        coef[r, 2] = wy
        coef[r, 3] = wyl
        coef[r, 4] = wz
        coef[r, 5] = wzl
        coef[r, 6] = (SHIFT - HELM) - (wx + wxl + wy + wyl + wz + wzl)
        coef[r, 7] = 0.25 * wide(r, A12)
        coef[r, 8] = 0.25 * wide(r, A13)
        coef[r, 9] = 0.25 * wide(r, A23)
        return 0

    lax.fori_loop(1, 13, make_coef, 0)

    wait_recv(half_r)

    def spread_rhs(j, tile, row):
        edge = pltpu.roll(tile, 128 - (8 * j + 4), 1)
        kry[0, row] = jnp.concatenate([rhs_rows[row], edge], axis=1)

    tile = jnp.where(from_left, rhs_beside[0], rhs_beside[1])
    for j in range(ny_dev):
        spread_rhs(j, tile, 3 + j)

    def halo_rhs(side, js, lo, inside):
        @pl.when(inside)
        def _():
            tile = jnp.where(from_left, rhs_corner[side, 0], rhs_corner[side, 1])
            for n, j in enumerate(js):
                spread_rhs(j, tile, lo + n)

        @pl.when(jnp.logical_not(inside))
        def _():
            for n in range(3):
                kry[0, lo + n] = jnp.zeros((nz, 256), jnp.float32)

    halo_rhs(0, (5, 6, 7), 0, gy > 0)
    halo_rhs(1, (0, 1, 2), 11, gy < ny - 1)

    def operate(n, r):
        p, up, down = kry[n, r], kry[n, r + 1], kry[n, r - 1]
        right, left = xp(p), xm(p)
        dx = right - left
        dy = up - down
        return (coef[r, 0] * right + coef[r, 1] * left + coef[r, 2] * up + coef[r, 3] * down
                + coef[r, 4] * zp(p) + coef[r, 5] * zm(p) + coef[r, 6] * p
                + coef[r, 7] * ((xp(up) - xm(up)) - (xp(down) - xm(down)))
                + coef[r, 8] * (zp(dx) - zm(dx)) + coef[r, 9] * (zp(dy) - zm(dy)))

    for n in range(2):
        def lift(r, _, n=n):
            kry[n + 1, r] = operate(n, r)
            return 0
        lax.fori_loop(1 + n, 13 - n, lift, 0)

    pairs = [(a, b) for a in range(ITERS + 1) for b in range(a, ITERS + 1)]

    def gram(r, acc):
        vecs = [kry[n, r][:, :128] for n in range(ITERS)] + [operate(ITERS - 1, r)[:, :128]]
        out = []
        for (a, b), s in zip(pairs, acc):
            prod = vecs[a] * vecs[b]
            out.append(s + (prod[:8] + prod[8:]))
        return tuple(out)

    sums = lax.fori_loop(3, 3 + ny_dev, gram, tuple(jnp.zeros((8, 128), jnp.float32) for _ in pairs))
    spot = lax.broadcasted_iota(jnp.int32, (16, 128), 0)
    tile = jnp.zeros((16, 128), jnp.float32)
    for n, s in enumerate(sums):
        tile = jnp.where(spot == n, jnp.sum(s, axis=0, keepdims=True), tile)
    part[...] = tile

    def x_copy(d):
        k = 28 + d - 1
        return pltpu.make_async_remote_copy(
            src_ref=part, dst_ref=part_x.at[d - 1], send_sem=send_sem.at[k], recv_sem=recv_sem.at[k],
            device_id={"gx": lax.rem(gx + d, nx), "gy": gy}, device_id_type=MESH)

    def y_copy(d):
        k = 28 + nx - 1 + d - 1
        return pltpu.make_async_remote_copy(
            src_ref=sum_x, dst_ref=part_y.at[d - 1], send_sem=send_sem.at[k], recv_sem=recv_sem.at[k],
            device_id={"gx": gx, "gy": lax.rem(gy + d, ny)}, device_id_type=MESH)

    for d in range(1, nx):
        x_copy(d).start()
    upwind(((3, TH),), 2, 12)
    for d in range(1, nx):
        x_copy(d).wait_recv()
    tile = part[...]
    for d in range(1, nx):
        tile = tile + part_x[d - 1]
    sum_x[...] = tile
    for d in range(1, ny):
        y_copy(d).start()
    antidiffuse((3,), 3, 11)

    def store(ref, base, j, value):
        ref[pl.ds(base + j, nz, stride=ny_dev), :] = value

    def put_theta(j, _):
        store(th_out, 0, j, second[3 + j, 3][:, :128])
        return 0

    lax.fori_loop(0, ny_dev, put_theta, 0)
    for d in range(1, ny):
        y_copy(d).wait_recv()
    tile = sum_x[...]
    for d in range(1, ny):
        tile = tile + part_y[d - 1]
    total = jnp.sum(tile, axis=1, keepdims=True)
    gmat = {}
    for n, (a, b) in enumerate(pairs):
        gmat[a, b] = gmat[b, a] = total[n:n + 1, :]

    def dot(a, b):
        terms = [x * y for x, y in zip(a, b) if x is not None and y is not None]
        return functools.reduce(lambda s, t: s + t, terms)

    def minus(a, s, b):
        out = []
        for x, y in zip(a, b):
            if y is None:
                out.append(x)
            else:
                out.append(-(s * y) if x is None else x - s * y)
        return out

    def image(a):
        out = [None if x is None else -SHIFT * x for x in a]
        for n in range(ITERS):
            if a[n] is not None:
                out[n + 1] = a[n] if out[n + 1] is None else out[n + 1] + a[n]
        return out

    one = jnp.ones((1, 1), jnp.float32)
    resid = [one] + [None] * ITERS
    dirs, images, duals, norms = [resid], [image(resid)], [], []
    press = [None] * (ITERS + 1)
    for step in range(ITERS):
        q = images[step]
        dual = [dot([gmat[a, b] for b in range(ITERS + 1)], q) for a in range(ITERS + 1)]
        duals.append(dual)
        norms.append(dot(q, dual))
        beta = dot(resid, dual) / norms[step]
        press = minus(press, -beta, dirs[step])
        if step + 1 < ITERS:
            resid = minus(resid, beta, q)
            lifted = image(resid)
            new_dir, new_img = resid, lifted
            for back in range(step + 1):
                alpha = dot(lifted, duals[back]) / norms[back]
                new_dir = minus(new_dir, alpha, dirs[back])
                new_img = minus(new_img, alpha, images[back])
            dirs.append(new_dir)
            images.append(new_img)
    c0, c1, c2 = [jnp.broadcast_to(c, (nz, 256)) for c in press[:ITERS]]

    def pressure(r):
        return c0 * kry[0, r] + c1 * kry[1, r] + c2 * kry[2, r]

    def finish(j, carry):
        down, here = carry
        r = 3 + j
        up = pressure(r + 1)
        store(p_out, 0, j, here[:, :128])
        store(mom_out, 0, j, (second[r, 0] - 0.5 * (xp(here) - xm(here)))[:, :128])
        store(mom_out, plane, j, (second[r, 1] - 0.5 * (up - down))[:, :128])
        store(mom_out, 2 * plane, j, (second[r, 2] - 0.5 * (zp(here) - zm(here)))[:, :128])
        return here, up

    lax.fori_loop(0, ny_dev, finish, (pressure(2), pressure(3)))

    wait_send(half_a)
    wait_send(half_b)
    wait_send(half_r)
    for d in range(1, nx):
        x_copy(d).wait_send()
    for d in range(1, ny):
        y_copy(d).wait_send()


def solution(mesh):
    nx, ny = mesh.shape["gx"], mesh.shape["gy"]

    def local(momenta, theta, courant, density, metric_diag, metric_cross):
        nz, ny_dev, nx_dev = density.shape
        args = (momenta, theta, courant, density, metric_diag, metric_cross)
        flat = [a.reshape(-1, nx_dev) for a in args]
        plane = nz * ny_dev
        f32 = jnp.float32
        n_ext = ny_dev + 6
        n_sem = 28 + nx - 1 + ny - 1
        shape = jax.ShapeDtypeStruct
        vmem = pltpu.VMEM
        mom, th, press = pl.pallas_call(
            functools.partial(kernel, nx, ny),
            out_shape=(shape((3 * plane, nx_dev), f32), shape((plane, nx_dev), f32),
                       shape((plane, nx_dev), f32)),
            in_specs=[pl.BlockSpec(memory_space=pl.ANY)] * 6,
            out_specs=[pl.BlockSpec(memory_space=pltpu.VMEM)] * 3,
            scratch_shapes=[
                vmem((14 * plane, nx_dev), f32),
                vmem((n_ext, 14, nz, nx_dev), f32),
                vmem((n_ext, 14, nz, nx_dev), f32),
                vmem((2, 4, nz, nx_dev), f32),
                vmem((2, 2, 4, nz, nx_dev), f32),
                vmem((2, 2, 2, 2, nz, nx_dev), f32),
                vmem((n_ext, 4, nz, 2 * nx_dev), f32),
                vmem((n_ext, 4, nz, 2 * nx_dev), f32),
                vmem((n_ext, 10, nz, 2 * nx_dev), f32),
                vmem((3, n_ext, nz, 2 * nx_dev), f32),
                vmem((n_ext, nz, nx_dev), f32),
                vmem((n_ext, nz, nx_dev), f32),
                vmem((nz, nx_dev), f32),
                vmem((2, nz, nx_dev), f32),
                vmem((2, 2, nz, nx_dev), f32),
                vmem((16, 128), f32),
                vmem((nx - 1, 16, 128), f32),
                vmem((16, 128), f32),
                vmem((ny - 1, 16, 128), f32),
                pltpu.SemaphoreType.DMA((6,)),
                pltpu.SemaphoreType.DMA((n_sem,)),
                pltpu.SemaphoreType.DMA((n_sem,)),
            ],
            compiler_params=pltpu.CompilerParams(
                collective_id=0, has_side_effects=True, vmem_limit_bytes=40 * 1024 * 1024),
        )(*flat)
        return mom.reshape(momenta.shape), th.reshape(theta.shape), press.reshape(theta.shape)

    placed = (
        P(None, None, "gy", "gx"),
        P(None, "gy", "gx"),
        P(None, None, "gy", "gx"),
        P(None, "gy", "gx"),
        P(None, None, "gy", "gx"),
        P(None, None, "gy", "gx"),
    )
    return jax.shard_map(
        local,
        mesh=mesh,
        in_specs=placed,
        out_specs=(P(None, None, "gy", "gx"), P(None, "gy", "gx"), P(None, "gy", "gx")),
        check_vma=False,
    )
```

```python
import functools

import jax
import jax.numpy as jnp
from jax import lax
from jax.experimental import pallas as pl
from jax.experimental.pallas import tpu as pltpu
from jax.sharding import PartitionSpec as P

ITERS = 3
HELM = 0.02
SHIFT = 6.0
MESH = pl.DeviceIdType.MESH

ORDER = (1, 5, 7, 0, 2, 4, 6, 9, 8, 10, 11, 12, 13, 3)
V, CY, RHO, U, W, CX, CZ, A22, A11, A33, A12, A13, A23, TH = range(14)
HALF = 7
THIRD = (2, 1)


def kernel(nx, ny, mom, theta, cour, dens, diag, cross, mom_out, th_out, p_out,
           cells, rows, edges, packed, beside, corner, first, second, coef,
           kry, rhs_rows, rhs_edges, rhs_packed, rhs_beside, rhs_corner,
           part, part_x, sum_x, part_y, in_sem, send_sem, recv_sem):
    gx = lax.axis_index("gx")
    gy = lax.axis_index("gy")
    nz = rows.shape[2]
    ny_dev = 8
    plane = nz * ny_dev

    def device(dx, dy):
        return {"gx": lax.rem(gx + dx + nx, nx), "gy": gy + dy}

    barrier = pltpu.get_barrier_semaphore()
    peers = [(lax.rem(gx + d, nx), gy) for d in range(1, nx)]
    peers += [(gx, lax.rem(gy + d, ny)) for d in range(1, ny)]
    peers += [(lax.rem(gx + a, nx), lax.rem(gy + b, ny)) for a in (1, nx - 1) for b in (1, ny - 1)]
    for a, b in peers:
        pl.semaphore_signal(barrier, inc=1, device_id={"gx": a, "gy": b}, device_id_type=MESH)

    loads = []
    place = 0
    for n, ref in enumerate((mom, theta, cour, dens, diag, cross)):
        size = ref.shape[0]
        loads.append(pltpu.make_async_copy(ref, cells.at[pl.ds(place, size)], in_sem.at[n]))
        place += size
    for n in (0, 2, 3, 1, 4, 5):
        loads[n].start()

    def clear(lo):
        rows[lo:lo + 3] = jnp.zeros((3,) + rows.shape[1:], jnp.float32)
        edges[lo:lo + 3] = jnp.zeros((3,) + edges.shape[1:], jnp.float32)
        for i in range(lo, lo + 3):
            rows[i, RHO] = jnp.ones(rows.shape[2:], jnp.float32)
            edges[i, RHO] = jnp.ones(rows.shape[2:], jnp.float32)
        rhs_rows[lo:lo + 3] = jnp.zeros((3,) + rhs_rows.shape[1:], jnp.float32)
        rhs_edges[lo:lo + 3] = jnp.zeros((3,) + rhs_edges.shape[1:], jnp.float32)

    pl.when(gy == 0)(lambda: clear(0))
    pl.when(gy == ny - 1)(lambda: clear(11))

    lane = lax.broadcasted_iota(jnp.int32, (nz, 128), 1)
    level = lax.broadcasted_iota(jnp.int32, (nz, 128), 0)
    slot = lane // 8
    from_left = lax.rem(lane, 8) < 4
    wide_level = lax.broadcasted_iota(jnp.int32, (nz, 256), 0)
    last = wide_level == nz - 1
    ground = wide_level == 0

    def xm(a):
        return pltpu.roll(a, 1, 1)

    def xp(a):
        return pltpu.roll(a, 255, 1)

    def zp(a):
        return jnp.where(last, 0.0, pltpu.roll(a, nz - 1, 0))

    def zm(a):
        return jnp.where(ground, 0.0, pltpu.roll(a, 1, 0))

    def grouped(lo, hi, size, body):
        count = (hi - lo) // size
        if count == 1:
            body(lo)
            return

        def step(n, _):
            body(lo + n * size)
            return 0
        lax.fori_loop(0, count, step, 0)

    def load_half(b):
        def some(j0):
            for j in (j0, j0 + 1):
                for f in range(b * HALF, b * HALF + HALF):
                    value = cells[pl.ds(ORDER[f] * plane + j, nz, stride=ny_dev), :]
                    if f == CY:
                        value = jnp.where(gy * ny_dev + j == 0, 0.0, value)
                    if f == CZ:
                        value = jnp.where(level == 0, 0.0, value)
                    rows[3 + j, f] = value
        grouped(0, ny_dev, 2, some)

    def pack_half(b):
        def one(t, _):
            acc = jnp.zeros((nz, 128), jnp.float32)
            for side in range(2):
                for fi in range(HALF):
                    p = 64 * side + 8 * fi
                    moved = pltpu.roll(rows[3 + 2 * t + side, b * HALF + fi], (p + 4) % 128, 1)
                    acc = jnp.where(slot == p // 8, moved, acc)
            packed[b, t] = acc
            return 0
        lax.fori_loop(0, ny_dev // 2, one, 0)

    def unpack_half(b):
        def spread(tile, side, row, count):
            for fi in range(count):
                p = 64 * side + 8 * fi
                edges[row, b * HALF + fi] = pltpu.roll(tile, (128 - (p + 4)) % 128, 1)

        def one(t, _):
            tile = jnp.where(from_left, beside[b, 0, t], beside[b, 1, t])
            for side in range(2):
                spread(tile, side, 3 + 2 * t + side, HALF)
            return 0
        lax.fori_loop(0, ny_dev // 2, one, 0)

        @pl.when(gy > 0)
        def _():
            for j in (5, 6, 7):
                tile = jnp.where(from_left, corner[b, 0, 0, j // 2 - 2], corner[b, 0, 1, j // 2 - 2])
                spread(tile, j % 2, j - 5, THIRD[b] if j == 5 else HALF)

        @pl.when(gy < ny - 1)
        def _():
            for j in (0, 1, 2):
                tile = jnp.where(from_left, corner[b, 1, 0, j // 2], corner[b, 1, 1, j // 2])
                spread(tile, j % 2, 11 + j, THIRD[b] if j == 2 else HALF)

    def remote(src, dst, k, dx, dy):
        return pltpu.make_async_remote_copy(
            src_ref=src, dst_ref=dst, send_sem=send_sem.at[k], recv_sem=recv_sem.at[k],
            device_id=device(dx, dy), device_id_type=MESH)

    def group(entries, base):
        by = {1: [], -1: [], 0: []}
        for n, (dx, dy, src, dst) in enumerate(entries):
            by[dy].append((src, dst, base + n, dx, dy))
        return by

    def each(by, action, sign):
        for dy in (1, -1, 0):
            def run(dy=dy):
                for item in by[dy]:
                    action(remote(*item))
            if dy == 0:
                run()
            elif dy * sign == 1:
                pl.when(gy < ny - 1)(run)
            else:
                pl.when(gy > 0)(run)

    def start(by):
        each(by, lambda c: c.start(), 1)

    def wait_recv(by):
        each(by, lambda c: c.wait_recv(), -1)

    def wait_send(by):
        each(by, lambda c: c.wait_send(), 1)

    def half_entries(b):
        fs = pl.ds(b * HALF, HALF)
        ft = pl.ds(b * HALF, THIRD[b])
        return [
            (0, 1, rows.at[pl.ds(9, 2), fs], rows.at[pl.ds(1, 2), fs]),
            (0, 1, rows.at[pl.ds(8, 1), ft], rows.at[pl.ds(0, 1), ft]),
            (0, -1, rows.at[pl.ds(3, 2), fs], rows.at[pl.ds(11, 2), fs]),
            (0, -1, rows.at[pl.ds(5, 1), ft], rows.at[pl.ds(13, 1), ft]),
            (1, 0, packed.at[b], beside.at[b, 0]),
            (-1, 0, packed.at[b], beside.at[b, 1]),
            (1, 1, packed.at[b, pl.ds(2, 2)], corner.at[b, 0, 0]),
            (-1, 1, packed.at[b, pl.ds(2, 2)], corner.at[b, 0, 1]),
            (1, -1, packed.at[b, pl.ds(0, 2)], corner.at[b, 1, 0]),
            (-1, -1, packed.at[b, pl.ds(0, 2)], corner.at[b, 1, 1]),
        ]

    half_a = group(half_entries(0), 0)
    half_b = group(half_entries(1), 10)
    half_r = group([
        (0, 1, rhs_rows.at[pl.ds(8, 3)], rhs_rows.at[pl.ds(0, 3)]),
        (0, -1, rhs_rows.at[pl.ds(3, 3)], rhs_rows.at[pl.ds(11, 3)]),
        (1, 0, rhs_packed, rhs_beside.at[0]),
        (-1, 0, rhs_packed, rhs_beside.at[1]),
        (1, 1, rhs_packed, rhs_corner.at[0, 0]),
        (-1, 1, rhs_packed, rhs_corner.at[0, 1]),
        (1, -1, rhs_packed, rhs_corner.at[1, 0]),
        (-1, -1, rhs_packed, rhs_corner.at[1, 1]),
    ], 20)

    for n in (0, 2, 3):
        loads[n].wait()
    load_half(0)
    pack_half(0)
    pl.semaphore_wait(barrier, len(peers))
    start(half_a)
    for n in (1, 4, 5):
        loads[n].wait()
    load_half(1)
    pack_half(1)
    start(half_b)

    def wide(r, f):
        return jnp.concatenate([rows[r, f], edges[r, f]], axis=1)

    def upwind(fields, lo, hi, size):
        def some(r0):
            span = range(size)
            cys = [wide(r0 + i, CY) for i in range(size + 1)]
            cys = [(jnp.maximum(c, 0.0), jnp.minimum(c, 0.0)) for c in cys]
            psi = {f: [wide(r0 + i - 1, f) for i in range(size + 2)] for _, f in fields}
            for i in span:
                r = r0 + i
                cx, cz = wide(r, CX), wide(r, CZ)
                inv = 1.0 / wide(r, RHO)
                cx_p, cx_n = jnp.maximum(cx, 0.0), jnp.minimum(cx, 0.0)
                cz_p, cz_n = jnp.maximum(cz, 0.0), jnp.minimum(cz, 0.0)
                for n, f in fields:
                    below, here, above = psi[f][i:i + 3]
                    fx = cx_p * xm(here) + cx_n * here
                    fz = cz_p * zm(here) + cz_n * here
                    fy = cys[i][0] * below + cys[i][1] * here
                    fu = cys[i + 1][0] * here + cys[i + 1][1] * above
                    total = xp(fx) - fx + fu - fy + zp(fz) - fz
                    first[r, n] = here - total * inv
        grouped(lo, hi, size, some)

    def face(c, a, b):
        return 0.5 * jnp.abs(c) - c * c / (a + b)

    def antidiffuse(fields, lo, hi, size):
        def some(r0):
            rhos = [wide(r0 + i - 1, RHO) for i in range(size + 2)]
            kys = [face(wide(r0 + i, CY), rhos[i], rhos[i + 1]) for i in range(size + 1)]
            for i in range(size):
                r = r0 + i
                rho = rhos[i + 1]
                inv = 1.0 / rho
                kx = face(wide(r, CX), xm(rho), rho)
                kz = face(wide(r, CZ), zm(rho), rho)
                for n in fields:
                    here = first[r, n]
                    ax = kx * (here - xm(here))
                    az = kz * (here - zm(here))
                    ay = kys[i] * (here - first[r - 1, n])
                    au = kys[i + 1] * (first[r + 1, n] - here)
                    total = xp(ax) - ax + au - ay + zp(az) - az
                    second[r, n] = here - total * inv
        grouped(lo, hi, size, some)

    wait_recv(half_a)
    unpack_half(0)
    upwind(((0, U), (1, V), (2, W)), 1, 13, 3)
    antidiffuse((0, 1, 2), 2, 12, 2)

    acc = jnp.zeros((nz, 128), jnp.float32)
    for j in range(ny_dev):
        r = 3 + j
        u, w = second[r, 0], second[r, 2]
        value = (0.5 * (xp(u) - xm(u)) + 0.5 * (second[r + 1, 1] - second[r - 1, 1])
                 + 0.5 * (zp(w) - zm(w)))[:, :128]
        rhs_rows[r] = value
        acc = jnp.where(slot == j, pltpu.roll(value, 8 * j + 4, 1), acc)
    rhs_packed[...] = acc
    start(half_r)

    wait_recv(half_b)
    unpack_half(1)

    def make_coef(r0):
        size = 4
        a22s = [wide(r0 + i - 1, A22) for i in range(size + 2)]
        wys = []
        for i in range(size + 1):
            at = gy * ny_dev + r0 + i - 3
            wys.append(jnp.where((at > 0) & (at < ny * ny_dev), 0.5 * (a22s[i] + a22s[i + 1]), 0.0))
        for i in range(size):
            r = r0 + i
            a11, a33 = wide(r, A11), wide(r, A33)
            wxl = 0.5 * (xm(a11) + a11)
            wx = xp(wxl)
            wyl, wy = wys[i], wys[i + 1]
            wzl = jnp.where(ground, 0.0, 0.5 * (zm(a33) + a33))
            wz = zp(wzl)
            coef[r, 0] = wx
            coef[r, 1] = wxl
            coef[r, 2] = wy
            coef[r, 3] = wyl
            coef[r, 4] = wz
            coef[r, 5] = wzl
            coef[r, 6] = (SHIFT - HELM) - (wx + wxl + wy + wyl + wz + wzl)
            coef[r, 7] = 0.25 * wide(r, A12)
            coef[r, 8] = 0.25 * wide(r, A13)
            coef[r, 9] = 0.25 * wide(r, A23)

    grouped(1, 13, 4, make_coef)

    wait_recv(half_r)

    def spread_rhs(j, tile, row):
        edge = pltpu.roll(tile, 128 - (8 * j + 4), 1)
        kry[0, row] = jnp.concatenate([rhs_rows[row], edge], axis=1)

    tile = jnp.where(from_left, rhs_beside[0], rhs_beside[1])
    for j in range(ny_dev):
        spread_rhs(j, tile, 3 + j)

    def halo_rhs(side, js, lo, inside):
        @pl.when(inside)
        def _():
            tile = jnp.where(from_left, rhs_corner[side, 0], rhs_corner[side, 1])
            for n, j in enumerate(js):
                spread_rhs(j, tile, lo + n)

        @pl.when(jnp.logical_not(inside))
        def _():
            for n in range(3):
                kry[0, lo + n] = jnp.zeros((nz, 256), jnp.float32)

    halo_rhs(0, (5, 6, 7), 0, gy > 0)
    halo_rhs(1, (0, 1, 2), 11, gy < ny - 1)

    def operate(n, r0, size):
        ps = [kry[n, r0 + i - 1] for i in range(size + 2)]
        sides = [(xp(p), xm(p)) for p in ps]
        dxs = [right - left for right, left in sides]
        out = []
        for i in range(size):
            r = r0 + i
            down, p, up = ps[i:i + 3]
            right, left = sides[i + 1]
            dx, dy = dxs[i + 1], up - down
            out.append(
                coef[r, 0] * right + coef[r, 1] * left + coef[r, 2] * up + coef[r, 3] * down
                + coef[r, 4] * zp(p) + coef[r, 5] * zm(p) + coef[r, 6] * p
                + coef[r, 7] * (dxs[i + 2] - dxs[i])
                + coef[r, 8] * (zp(dx) - zm(dx)) + coef[r, 9] * (zp(dy) - zm(dy)))
        return out

    for n, size in ((0, 4), (1, 5)):
        def lift(r0, n=n, size=size):
            for i, value in enumerate(operate(n, r0, size)):
                kry[n + 1, r0 + i] = value
        grouped(1 + n, 13 - n, size, lift)

    pairs = [(a, b) for a in range(ITERS + 1) for b in range(a, ITERS + 1)]

    def gram(step, acc):
        r0 = 3 + 4 * step
        tops = operate(ITERS - 1, r0, 4)
        acc = list(acc)
        for i in range(4):
            vecs = [kry[n, r0 + i][:, :128] for n in range(ITERS)] + [tops[i][:, :128]]
            for n, (a, b) in enumerate(pairs):
                prod = vecs[a] * vecs[b]
                acc[n] = acc[n] + (prod[:8] + prod[8:])
        return tuple(acc)

    sums = lax.fori_loop(0, ny_dev // 4, gram, tuple(jnp.zeros((8, 128), jnp.float32) for _ in pairs))
    spot = lax.broadcasted_iota(jnp.int32, (16, 128), 0)
    tile = jnp.zeros((16, 128), jnp.float32)
    for n, s in enumerate(sums):
        tile = jnp.where(spot == n, jnp.sum(s, axis=0, keepdims=True), tile)
    part[...] = tile

    def x_copy(d):
        k = 28 + d - 1
        return pltpu.make_async_remote_copy(
            src_ref=part, dst_ref=part_x.at[d - 1], send_sem=send_sem.at[k], recv_sem=recv_sem.at[k],
            device_id={"gx": lax.rem(gx + d, nx), "gy": gy}, device_id_type=MESH)

    def y_copy(d):
        k = 28 + nx - 1 + d - 1
        return pltpu.make_async_remote_copy(
            src_ref=sum_x, dst_ref=part_y.at[d - 1], send_sem=send_sem.at[k], recv_sem=recv_sem.at[k],
            device_id={"gx": gx, "gy": lax.rem(gy + d, ny)}, device_id_type=MESH)

    for d in range(1, nx):
        x_copy(d).start()
    upwind(((3, TH),), 2, 12, 5)
    for d in range(1, nx):
        x_copy(d).wait_recv()
    tile = part[...]
    for d in range(1, nx):
        tile = tile + part_x[d - 1]
    sum_x[...] = tile
    for d in range(1, ny):
        y_copy(d).start()
    antidiffuse((3,), 3, 11, 4)

    def store(ref, base, j, value):
        ref[pl.ds(base + j, nz, stride=ny_dev), :] = value

    for j in range(ny_dev):
        store(th_out, 0, j, second[3 + j, 3][:, :128])
    for d in range(1, ny):
        y_copy(d).wait_recv()
    tile = sum_x[...]
    for d in range(1, ny):
        tile = tile + part_y[d - 1]
    total = jnp.sum(tile, axis=1, keepdims=True)
    gmat = {}
    for n, (a, b) in enumerate(pairs):
        gmat[a, b] = gmat[b, a] = total[n:n + 1, :]

    def dot(a, b):
        terms = [x * y for x, y in zip(a, b) if x is not None and y is not None]
        return functools.reduce(lambda s, t: s + t, terms)

    def minus(a, s, b):
        out = []
        for x, y in zip(a, b):
            if y is None:
                out.append(x)
            else:
                out.append(-(s * y) if x is None else x - s * y)
        return out

    def image(a):
        out = [None if x is None else -SHIFT * x for x in a]
        for n in range(ITERS):
            if a[n] is not None:
                out[n + 1] = a[n] if out[n + 1] is None else out[n + 1] + a[n]
        return out

    one = jnp.ones((1, 1), jnp.float32)
    resid = [one] + [None] * ITERS
    dirs, images, duals, norms = [resid], [image(resid)], [], []
    press = [None] * (ITERS + 1)
    for step in range(ITERS):
        q = images[step]
        dual = [dot([gmat[a, b] for b in range(ITERS + 1)], q) for a in range(ITERS + 1)]
        duals.append(dual)
        norms.append(dot(q, dual))
        beta = dot(resid, dual) / norms[step]
        press = minus(press, -beta, dirs[step])
        if step + 1 < ITERS:
            resid = minus(resid, beta, q)
            lifted = image(resid)
            new_dir, new_img = resid, lifted
            for back in range(step + 1):
                alpha = dot(lifted, duals[back]) / norms[back]
                new_dir = minus(new_dir, alpha, dirs[back])
                new_img = minus(new_img, alpha, images[back])
            dirs.append(new_dir)
            images.append(new_img)
    c0, c1, c2 = [jnp.broadcast_to(c, (nz, 256)) for c in press[:ITERS]]

    def pressure(r):
        return c0 * kry[0, r] + c1 * kry[1, r] + c2 * kry[2, r]

    def finish(j0):
        size = 4
        ps = [pressure(3 + j0 + i - 1) for i in range(size + 2)]
        for i in range(size):
            j = j0 + i
            r = 3 + j
            down, here, up = ps[i:i + 3]
            store(p_out, 0, j, here[:, :128])
            store(mom_out, 0, j, (second[r, 0] - 0.5 * (xp(here) - xm(here)))[:, :128])
            store(mom_out, plane, j, (second[r, 1] - 0.5 * (up - down))[:, :128])
            store(mom_out, 2 * plane, j, (second[r, 2] - 0.5 * (zp(here) - zm(here)))[:, :128])

    grouped(0, ny_dev, 4, finish)

    wait_send(half_a)
    wait_send(half_b)
    wait_send(half_r)
    for d in range(1, nx):
        x_copy(d).wait_send()
    for d in range(1, ny):
        y_copy(d).wait_send()


def solution(mesh):
    nx, ny = mesh.shape["gx"], mesh.shape["gy"]

    def local(momenta, theta, courant, density, metric_diag, metric_cross):
        nz, ny_dev, nx_dev = density.shape
        args = (momenta, theta, courant, density, metric_diag, metric_cross)
        flat = [a.reshape(-1, nx_dev) for a in args]
        plane = nz * ny_dev
        f32 = jnp.float32
        n_ext = ny_dev + 6
        n_sem = 28 + nx - 1 + ny - 1
        shape = jax.ShapeDtypeStruct
        vmem = pltpu.VMEM
        mom, th, press = pl.pallas_call(
            functools.partial(kernel, nx, ny),
            out_shape=(shape((3 * plane, nx_dev), f32), shape((plane, nx_dev), f32),
                       shape((plane, nx_dev), f32)),
            in_specs=[pl.BlockSpec(memory_space=pltpu.HBM)] * 6,
            out_specs=[pl.BlockSpec(memory_space=pltpu.VMEM)] * 3,
            scratch_shapes=[
                vmem((14 * plane, nx_dev), f32),
                vmem((n_ext, 14, nz, nx_dev), f32),
                vmem((n_ext, 14, nz, nx_dev), f32),
                vmem((2, 4, nz, nx_dev), f32),
                vmem((2, 2, 4, nz, nx_dev), f32),
                vmem((2, 2, 2, 2, nz, nx_dev), f32),
                vmem((n_ext, 4, nz, 2 * nx_dev), f32),
                vmem((n_ext, 4, nz, 2 * nx_dev), f32),
                vmem((n_ext, 10, nz, 2 * nx_dev), f32),
                vmem((3, n_ext, nz, 2 * nx_dev), f32),
                vmem((n_ext, nz, nx_dev), f32),
                vmem((n_ext, nz, nx_dev), f32),
                vmem((nz, nx_dev), f32),
                vmem((2, nz, nx_dev), f32),
                vmem((2, 2, nz, nx_dev), f32),
                vmem((16, 128), f32),
                vmem((nx - 1, 16, 128), f32),
                vmem((16, 128), f32),
                vmem((ny - 1, 16, 128), f32),
                pltpu.SemaphoreType.DMA((6,)),
                pltpu.SemaphoreType.DMA((n_sem,)),
                pltpu.SemaphoreType.DMA((n_sem,)),
            ],
            compiler_params=pltpu.CompilerParams(
                collective_id=0, has_side_effects=True, vmem_limit_bytes=60 * 1024 * 1024),
        )(*flat)
        return mom.reshape(momenta.shape), th.reshape(theta.shape), press.reshape(theta.shape)

    placed = (
        P(None, None, "gy", "gx"),
        P(None, "gy", "gx"),
        P(None, None, "gy", "gx"),
        P(None, "gy", "gx"),
        P(None, None, "gy", "gx"),
        P(None, None, "gy", "gx"),
    )
    return jax.shard_map(
        local,
        mesh=mesh,
        in_specs=placed,
        out_specs=(P(None, None, "gy", "gx"), P(None, "gy", "gx"), P(None, "gy", "gx")),
        check_vma=False,
    )
```

```python
import functools

import jax
import jax.numpy as jnp
from jax import lax
from jax.experimental import pallas as pl
from jax.experimental.pallas import tpu as pltpu
from jax.sharding import PartitionSpec as P

ITERS = 3
HELM = 0.02
SHIFT = 6.0
MESH = pl.DeviceIdType.MESH

ORDER = (1, 5, 7, 0, 2, 4, 6, 9, 8, 10, 11, 12, 13, 3)
V, CY, RHO, U, W, CX, CZ, A22, A11, A33, A12, A13, A23, TH = range(14)
HALF = 7
THIRD = (2, 1)


def kernel(nx, ny, mom, theta, cour, dens, diag, cross, mom_out, th_out, p_out,
           cells, rows, edges, packed, beside, corner, first, second, coef,
           kry, rhs_rows, rhs_packed, rhs_beside, rhs_corner,
           part, part_x, sum_x, part_y, in_sem, send_sem, recv_sem):
    gx = lax.axis_index("gx")
    gy = lax.axis_index("gy")
    nz = rows.shape[2]
    ny_dev = 8
    plane = nz * ny_dev

    def device(dx, dy):
        return {"gx": lax.rem(gx + dx + nx, nx), "gy": gy + dy}

    barrier = pltpu.get_barrier_semaphore()
    peers = [(lax.rem(gx + d, nx), gy) for d in range(1, nx)]
    peers += [(gx, lax.rem(gy + d, ny)) for d in range(1, ny)]
    peers += [(lax.rem(gx + a, nx), lax.rem(gy + b, ny)) for a in (1, nx - 1) for b in (1, ny - 1)]
    for a, b in peers:
        pl.semaphore_signal(barrier, inc=1, device_id={"gx": a, "gy": b}, device_id_type=MESH)

    loads = []
    place = 0
    for n, ref in enumerate((mom, theta, cour, dens, diag, cross)):
        size = ref.shape[0]
        loads.append(pltpu.make_async_copy(ref, cells.at[pl.ds(place, size)], in_sem.at[n]))
        place += size
    for n in (0, 2, 3, 1, 4, 5):
        loads[n].start()

    def clear(lo):
        rows[lo:lo + 3] = jnp.zeros((3,) + rows.shape[1:], jnp.float32)
        edges[lo:lo + 3] = jnp.zeros((3,) + edges.shape[1:], jnp.float32)
        for i in range(lo, lo + 3):
            rows[i, RHO] = jnp.ones(rows.shape[2:], jnp.float32)
            edges[i, RHO] = jnp.ones(rows.shape[2:], jnp.float32)
        rhs_rows[lo:lo + 3] = jnp.zeros((3,) + rhs_rows.shape[1:], jnp.float32)

    pl.when(gy == 0)(lambda: clear(0))
    pl.when(gy == ny - 1)(lambda: clear(11))

    lane = lax.broadcasted_iota(jnp.int32, (nz, 128), 1)
    level = lax.broadcasted_iota(jnp.int32, (nz, 128), 0)
    slot = lane // 8
    from_left = lax.rem(lane, 8) < 4
    wide_level = lax.broadcasted_iota(jnp.int32, (nz, 256), 0)
    last = wide_level == nz - 1
    ground = wide_level == 0

    def xm(a):
        return pltpu.roll(a, 1, 1)

    def xp(a):
        return pltpu.roll(a, 255, 1)

    def zp(a):
        return jnp.where(last, 0.0, pltpu.roll(a, nz - 1, 0))

    def zm(a):
        return jnp.where(ground, 0.0, pltpu.roll(a, 1, 0))

    def grouped(lo, hi, size, body, stride=None):
        stride = size if stride is None else stride
        count = (hi - lo) // stride
        if count == 1:
            body(lo)
            return

        def step(n, _):
            body(lo + n * stride)
            return 0
        lax.fori_loop(0, count, step, 0)

    def load_half(b):
        def some(j0):
            for j in (j0, j0 + 1):
                for f in range(b * HALF, b * HALF + HALF):
                    value = cells[pl.ds(ORDER[f] * plane + j, nz, stride=ny_dev), :]
                    if f == CY:
                        value = jnp.where(gy * ny_dev + j == 0, 0.0, value)
                    if f == CZ:
                        value = jnp.where(level == 0, 0.0, value)
                    rows[3 + j, f] = value
        grouped(0, ny_dev, 2, some)

    def pack_half(b):
        def one(t, _):
            acc = jnp.zeros((nz, 128), jnp.float32)
            for side in range(2):
                for fi in range(HALF):
                    p = 64 * side + 8 * fi
                    moved = pltpu.roll(rows[3 + 2 * t + side, b * HALF + fi], (p + 4) % 128, 1)
                    acc = jnp.where(slot == p // 8, moved, acc)
            for fi in range(THIRD[b]):
                p = 56 + 64 * fi
                moved = pltpu.roll(rows[5 + 3 * (t // 2), b * HALF + fi], (p + 4) % 128, 1)
                acc = jnp.where(slot == p // 8, moved, acc)
            packed[b, t] = acc
            return 0
        lax.fori_loop(0, ny_dev // 2, one, 0)

    def spread(b, tile, side, row):
        for fi in range(HALF):
            p = 64 * side + 8 * fi
            edges[row, b * HALF + fi] = pltpu.roll(tile, (128 - (p + 4)) % 128, 1)

    def unpack_own(b):
        def one(t, _):
            tile = jnp.where(from_left, beside[b, 0, t], beside[b, 1, t])
            for side in range(2):
                spread(b, tile, side, 3 + 2 * t + side)
            return 0
        lax.fori_loop(0, ny_dev // 2, one, 0)

    def unpack_halo(b):
        def one(side, near, third):
            tile = jnp.where(from_left, corner[b, side, 0], corner[b, side, 1])
            spread(b, tile, 0, near)
            spread(b, tile, 1, near + 1)
            for fi in range(THIRD[b]):
                edges[third, b * HALF + fi] = pltpu.roll(tile, (128 - (60 + 64 * fi)) % 128, 1)

        pl.when(gy > 0)(lambda: one(0, 1, 0))
        pl.when(gy < ny - 1)(lambda: one(1, 11, 13))

    def remote(src, dst, k, dx, dy):
        return pltpu.make_async_remote_copy(
            src_ref=src, dst_ref=dst, send_sem=send_sem.at[k], recv_sem=recv_sem.at[k],
            device_id=device(dx, dy), device_id_type=MESH)

    def group(entries, base):
        by = {1: [], -1: [], 0: []}
        for n, (dx, dy, src, dst) in enumerate(entries):
            by[dy].append((src, dst, base + n, dx, dy))
        return by

    def each(by, action, sign, order=(0, 1, -1)):
        for dy in order:
            def run(dy=dy):
                for item in by[dy]:
                    action(remote(*item))
            if dy == 0:
                run()
            elif dy * sign == 1:
                pl.when(gy < ny - 1)(run)
            else:
                pl.when(gy > 0)(run)

    def start(by):
        each(by, lambda c: c.start(), 1)

    def wait_beside(by):
        each(by, lambda c: c.wait_recv(), -1, (0,))

    def wait_halo(by):
        each(by, lambda c: c.wait_recv(), -1, (1, -1))

    def wait_send(by):
        each(by, lambda c: c.wait_send(), 1)

    def half_entries(b):
        fs = pl.ds(b * HALF, HALF)
        ft = pl.ds(b * HALF, THIRD[b])
        return [
            (0, 1, rows.at[pl.ds(9, 2), fs], rows.at[pl.ds(1, 2), fs]),
            (0, 1, rows.at[pl.ds(8, 1), ft], rows.at[pl.ds(0, 1), ft]),
            (0, -1, rows.at[pl.ds(3, 2), fs], rows.at[pl.ds(11, 2), fs]),
            (0, -1, rows.at[pl.ds(5, 1), ft], rows.at[pl.ds(13, 1), ft]),
            (1, 0, packed.at[b], beside.at[b, 0]),
            (-1, 0, packed.at[b], beside.at[b, 1]),
            (1, 1, packed.at[b, 3], corner.at[b, 0, 0]),
            (-1, 1, packed.at[b, 3], corner.at[b, 0, 1]),
            (1, -1, packed.at[b, 0], corner.at[b, 1, 0]),
            (-1, -1, packed.at[b, 0], corner.at[b, 1, 1]),
        ]

    half_a = group(half_entries(0), 0)
    half_b = group(half_entries(1), 10)
    half_r = group([
        (0, 1, rhs_rows.at[pl.ds(8, 3)], rhs_rows.at[pl.ds(0, 3)]),
        (0, -1, rhs_rows.at[pl.ds(3, 3)], rhs_rows.at[pl.ds(11, 3)]),
        (1, 0, rhs_packed, rhs_beside.at[0]),
        (-1, 0, rhs_packed, rhs_beside.at[1]),
        (1, 1, rhs_packed, rhs_corner.at[0, 0]),
        (-1, 1, rhs_packed, rhs_corner.at[0, 1]),
        (1, -1, rhs_packed, rhs_corner.at[1, 0]),
        (-1, -1, rhs_packed, rhs_corner.at[1, 1]),
    ], 20)

    for n in (0, 2, 3):
        loads[n].wait()
    load_half(0)
    pack_half(0)
    pl.semaphore_wait(barrier, len(peers))
    start(half_a)
    for n in (1, 4, 5):
        loads[n].wait()
    load_half(1)
    pack_half(1)
    start(half_b)

    def wide(r, f):
        return jnp.concatenate([rows[r, f], edges[r, f]], axis=1)

    def upwind(fields, lo, hi, size, stride=None):
        def some(r0):
            span = range(size)
            cys = [wide(r0 + i, CY) for i in range(size + 1)]
            cys = [(jnp.maximum(c, 0.0), jnp.minimum(c, 0.0)) for c in cys]
            psi = {f: [wide(r0 + i - 1, f) for i in range(size + 2)] for _, f in fields}
            for i in span:
                r = r0 + i
                cx, cz = wide(r, CX), wide(r, CZ)
                inv = 1.0 / wide(r, RHO)
                cx_p, cx_n = jnp.maximum(cx, 0.0), jnp.minimum(cx, 0.0)
                cz_p, cz_n = jnp.maximum(cz, 0.0), jnp.minimum(cz, 0.0)
                for n, f in fields:
                    below, here, above = psi[f][i:i + 3]
                    fx = cx_p * xm(here) + cx_n * here
                    fz = cz_p * zm(here) + cz_n * here
                    fy = cys[i][0] * below + cys[i][1] * here
                    fu = cys[i + 1][0] * here + cys[i + 1][1] * above
                    total = xp(fx) - fx + fu - fy + zp(fz) - fz
                    first[r, n] = here - total * inv
        grouped(lo, hi, size, some, stride)

    def face(c, a, b):
        return 0.5 * jnp.abs(c) - c * c / (a + b)

    def antidiffuse(fields, lo, hi, size, stride=None):
        def some(r0):
            rhos = [wide(r0 + i - 1, RHO) for i in range(size + 2)]
            kys = [face(wide(r0 + i, CY), rhos[i], rhos[i + 1]) for i in range(size + 1)]
            for i in range(size):
                r = r0 + i
                rho = rhos[i + 1]
                inv = 1.0 / rho
                kx = face(wide(r, CX), xm(rho), rho)
                kz = face(wide(r, CZ), zm(rho), rho)
                for n in fields:
                    here = first[r, n]
                    ax = kx * (here - xm(here))
                    az = kz * (here - zm(here))
                    ay = kys[i] * (here - first[r - 1, n])
                    au = kys[i + 1] * (first[r + 1, n] - here)
                    total = xp(ax) - ax + au - ay + zp(az) - az
                    second[r, n] = here - total * inv
        grouped(lo, hi, size, some, stride)

    wind = ((0, U), (1, V), (2, W))
    wait_beside(half_a)
    unpack_own(0)
    upwind(wind, 4, 10, 3)
    antidiffuse((0, 1, 2), 5, 9, 2)
    wait_halo(half_a)
    unpack_halo(0)
    upwind(wind, 1, 19, 3, 9)
    antidiffuse((0, 1, 2), 2, 16, 3, 7)

    acc = jnp.zeros((nz, 128), jnp.float32)
    for j in range(ny_dev):
        r = 3 + j
        u, w = second[r, 0], second[r, 2]
        value = (0.5 * (xp(u) - xm(u)) + 0.5 * (second[r + 1, 1] - second[r - 1, 1])
                 + 0.5 * (zp(w) - zm(w)))[:, :128]
        rhs_rows[r] = value
        acc = jnp.where(slot == j, pltpu.roll(value, 8 * j + 4, 1), acc)
    rhs_packed[...] = acc
    start(half_r)

    wait_beside(half_b)
    unpack_own(1)
    wait_halo(half_b)
    unpack_halo(1)

    def make_coef(r0):
        size = 4
        a22s = [wide(r0 + i - 1, A22) for i in range(size + 2)]
        wys = []
        for i in range(size + 1):
            at = gy * ny_dev + r0 + i - 3
            wys.append(jnp.where((at > 0) & (at < ny * ny_dev), 0.5 * (a22s[i] + a22s[i + 1]), 0.0))
        for i in range(size):
            r = r0 + i
            a11, a33 = wide(r, A11), wide(r, A33)
            wxl = 0.5 * (xm(a11) + a11)
            wx = xp(wxl)
            wyl, wy = wys[i], wys[i + 1]
            wzl = jnp.where(ground, 0.0, 0.5 * (zm(a33) + a33))
            wz = zp(wzl)
            coef[r, 0] = wx
            coef[r, 1] = wxl
            coef[r, 2] = wy
            coef[r, 3] = wyl
            coef[r, 4] = wz
            coef[r, 5] = wzl
            coef[r, 6] = (SHIFT - HELM) - (wx + wxl + wy + wyl + wz + wzl)
            coef[r, 7] = 0.25 * wide(r, A12)
            coef[r, 8] = 0.25 * wide(r, A13)
            coef[r, 9] = 0.25 * wide(r, A23)

    grouped(1, 13, 4, make_coef)

    def spread_rhs(j, tile, row):
        edge = pltpu.roll(tile, 128 - (8 * j + 4), 1)
        kry[0, row] = jnp.concatenate([rhs_rows[row], edge], axis=1)

    def halo_rhs(side, js, lo, inside):
        @pl.when(inside)
        def _():
            tile = jnp.where(from_left, rhs_corner[side, 0], rhs_corner[side, 1])
            for n, j in enumerate(js):
                spread_rhs(j, tile, lo + n)

        @pl.when(jnp.logical_not(inside))
        def _():
            for n in range(3):
                kry[0, lo + n] = jnp.zeros((nz, 256), jnp.float32)

    def operate(n, r0, size):
        ps = [kry[n, r0 + i - 1] for i in range(size + 2)]
        sides = [(xp(p), xm(p)) for p in ps]
        dxs = [right - left for right, left in sides]
        out = []
        for i in range(size):
            r = r0 + i
            down, p, up = ps[i:i + 3]
            right, left = sides[i + 1]
            dx, dy = dxs[i + 1], up - down
            out.append(
                coef[r, 0] * right + coef[r, 1] * left + coef[r, 2] * up + coef[r, 3] * down
                + coef[r, 4] * zp(p) + coef[r, 5] * zm(p) + coef[r, 6] * p
                + coef[r, 7] * (dxs[i + 2] - dxs[i])
                + coef[r, 8] * (zp(dx) - zm(dx)) + coef[r, 9] * (zp(dy) - zm(dy)))
        return out

    def lift(n, lo, hi, size, stride=None):
        def some(r0):
            for i, value in enumerate(operate(n, r0, size)):
                kry[n + 1, r0 + i] = value
        grouped(lo, hi, size, some, stride)

    pairs = [(a, b) for a in range(ITERS + 1) for b in range(a, ITERS + 1)]

    def gram(acc, r0, size):
        tops = operate(ITERS - 1, r0, size)
        acc = list(acc)
        for i in range(size):
            vecs = [kry[n, r0 + i][:, :128] for n in range(ITERS)] + [tops[i][:, :128]]
            for n, (a, b) in enumerate(pairs):
                prod = vecs[a] * vecs[b]
                acc[n] = acc[n] + (prod[:8] + prod[8:])
        return tuple(acc)

    wait_beside(half_r)
    tile = jnp.where(from_left, rhs_beside[0], rhs_beside[1])
    for j in range(ny_dev):
        spread_rhs(j, tile, 3 + j)
    lift(0, 4, 10, 3)
    lift(1, 5, 9, 4)
    sums = gram(tuple(jnp.zeros((8, 128), jnp.float32) for _ in pairs), 6, 2)
    wait_halo(half_r)
    halo_rhs(0, (5, 6, 7), 0, gy > 0)
    halo_rhs(1, (0, 1, 2), 11, gy < ny - 1)
    lift(0, 1, 19, 3, 9)
    lift(1, 2, 16, 3, 7)
    sums = lax.fori_loop(0, 2, lambda n, acc: gram(acc, 3 + 5 * n, 3), sums)
    spot = lax.broadcasted_iota(jnp.int32, (16, 128), 0)
    tile = jnp.zeros((16, 128), jnp.float32)
    for n, s in enumerate(sums):
        tile = jnp.where(spot == n, jnp.sum(s, axis=0, keepdims=True), tile)
    part[...] = tile

    def x_copy(d):
        k = 28 + d - 1
        return pltpu.make_async_remote_copy(
            src_ref=part, dst_ref=part_x.at[d - 1], send_sem=send_sem.at[k], recv_sem=recv_sem.at[k],
            device_id={"gx": lax.rem(gx + d, nx), "gy": gy}, device_id_type=MESH)

    def y_copy(d):
        k = 28 + nx - 1 + d - 1
        return pltpu.make_async_remote_copy(
            src_ref=sum_x, dst_ref=part_y.at[d - 1], send_sem=send_sem.at[k], recv_sem=recv_sem.at[k],
            device_id={"gx": gx, "gy": lax.rem(gy + d, ny)}, device_id_type=MESH)

    for d in range(1, nx):
        x_copy(d).start()
    upwind(((3, TH),), 2, 12, 5)
    for d in range(1, nx):
        x_copy(d).wait_recv()
    tile = part[...]
    for d in range(1, nx):
        tile = tile + part_x[d - 1]
    sum_x[...] = tile
    for d in range(1, ny):
        y_copy(d).start()
    antidiffuse((3,), 3, 11, 4)

    def store(ref, base, j, value):
        ref[pl.ds(base + j, nz, stride=ny_dev), :] = value

    for j in range(ny_dev):
        store(th_out, 0, j, second[3 + j, 3][:, :128])
    for d in range(1, ny):
        y_copy(d).wait_recv()
    tile = sum_x[...]
    for d in range(1, ny):
        tile = tile + part_y[d - 1]
    total = jnp.sum(tile, axis=1, keepdims=True)
    gmat = {}
    for n, (a, b) in enumerate(pairs):
        gmat[a, b] = gmat[b, a] = total[n:n + 1, :]

    def dot(a, b):
        terms = [x * y for x, y in zip(a, b) if x is not None and y is not None]
        return functools.reduce(lambda s, t: s + t, terms)

    def minus(a, s, b):
        out = []
        for x, y in zip(a, b):
            if y is None:
                out.append(x)
            else:
                out.append(-(s * y) if x is None else x - s * y)
        return out

    def image(a):
        out = [None if x is None else -SHIFT * x for x in a]
        for n in range(ITERS):
            if a[n] is not None:
                out[n + 1] = a[n] if out[n + 1] is None else out[n + 1] + a[n]
        return out

    one = jnp.ones((1, 1), jnp.float32)
    resid = [one] + [None] * ITERS
    dirs, images, duals, norms = [resid], [image(resid)], [], []
    press = [None] * (ITERS + 1)
    for step in range(ITERS):
        q = images[step]
        dual = [dot([gmat[a, b] for b in range(ITERS + 1)], q) for a in range(ITERS + 1)]
        duals.append(dual)
        norms.append(dot(q, dual))
        beta = dot(resid, dual) / norms[step]
        press = minus(press, -beta, dirs[step])
        if step + 1 < ITERS:
            resid = minus(resid, beta, q)
            lifted = image(resid)
            new_dir, new_img = resid, lifted
            for back in range(step + 1):
                alpha = dot(lifted, duals[back]) / norms[back]
                new_dir = minus(new_dir, alpha, dirs[back])
                new_img = minus(new_img, alpha, images[back])
            dirs.append(new_dir)
            images.append(new_img)
    c0, c1, c2 = [jnp.broadcast_to(c, (nz, 256)) for c in press[:ITERS]]

    def pressure(r):
        return c0 * kry[0, r] + c1 * kry[1, r] + c2 * kry[2, r]

    def finish(j0):
        size = 4
        ps = [pressure(3 + j0 + i - 1) for i in range(size + 2)]
        for i in range(size):
            j = j0 + i
            r = 3 + j
            down, here, up = ps[i:i + 3]
            store(p_out, 0, j, here[:, :128])
            store(mom_out, 0, j, (second[r, 0] - 0.5 * (xp(here) - xm(here)))[:, :128])
            store(mom_out, plane, j, (second[r, 1] - 0.5 * (up - down))[:, :128])
            store(mom_out, 2 * plane, j, (second[r, 2] - 0.5 * (zp(here) - zm(here)))[:, :128])

    grouped(0, ny_dev, 4, finish)

    wait_send(half_a)
    wait_send(half_b)
    wait_send(half_r)
    for d in range(1, nx):
        x_copy(d).wait_send()
    for d in range(1, ny):
        y_copy(d).wait_send()


def solution(mesh):
    nx, ny = mesh.shape["gx"], mesh.shape["gy"]

    def local(momenta, theta, courant, density, metric_diag, metric_cross):
        nz, ny_dev, nx_dev = density.shape
        args = (momenta, theta, courant, density, metric_diag, metric_cross)
        flat = [a.reshape(-1, nx_dev) for a in args]
        plane = nz * ny_dev
        f32 = jnp.float32
        n_ext = ny_dev + 6
        n_sem = 28 + nx - 1 + ny - 1
        shape = jax.ShapeDtypeStruct
        vmem = pltpu.VMEM
        mom, th, press = pl.pallas_call(
            functools.partial(kernel, nx, ny),
            out_shape=(shape((3 * plane, nx_dev), f32), shape((plane, nx_dev), f32),
                       shape((plane, nx_dev), f32)),
            in_specs=[pl.BlockSpec(memory_space=pltpu.HBM)] * 6,
            out_specs=[pl.BlockSpec(memory_space=pltpu.VMEM)] * 3,
            scratch_shapes=[
                vmem((14 * plane, nx_dev), f32),
                vmem((n_ext, 14, nz, nx_dev), f32),
                vmem((n_ext, 14, nz, nx_dev), f32),
                vmem((2, 4, nz, nx_dev), f32),
                vmem((2, 2, 4, nz, nx_dev), f32),
                vmem((2, 2, 2, nz, nx_dev), f32),
                vmem((n_ext, 4, nz, 2 * nx_dev), f32),
                vmem((n_ext, 4, nz, 2 * nx_dev), f32),
                vmem((n_ext, 10, nz, 2 * nx_dev), f32),
                vmem((3, n_ext, nz, 2 * nx_dev), f32),
                vmem((n_ext, nz, nx_dev), f32),
                vmem((nz, nx_dev), f32),
                vmem((2, nz, nx_dev), f32),
                vmem((2, 2, nz, nx_dev), f32),
                vmem((16, 128), f32),
                vmem((nx - 1, 16, 128), f32),
                vmem((16, 128), f32),
                vmem((ny - 1, 16, 128), f32),
                pltpu.SemaphoreType.DMA((6,)),
                pltpu.SemaphoreType.DMA((n_sem,)),
                pltpu.SemaphoreType.DMA((n_sem,)),
            ],
            compiler_params=pltpu.CompilerParams(
                collective_id=0, has_side_effects=True, vmem_limit_bytes=60 * 1024 * 1024),
        )(*flat)
        return mom.reshape(momenta.shape), th.reshape(theta.shape), press.reshape(theta.shape)

    placed = (
        P(None, None, "gy", "gx"),
        P(None, "gy", "gx"),
        P(None, None, "gy", "gx"),
        P(None, "gy", "gx"),
        P(None, None, "gy", "gx"),
        P(None, None, "gy", "gx"),
    )
    return jax.shard_map(
        local,
        mesh=mesh,
        in_specs=placed,
        out_specs=(P(None, None, "gy", "gx"), P(None, "gy", "gx"), P(None, "gy", "gx")),
        check_vma=False,
    )
```

```python
import functools

import jax
import jax.numpy as jnp
from jax import lax
from jax.experimental import pallas as pl
from jax.experimental.pallas import tpu as pltpu
from jax.sharding import PartitionSpec as P

ITERS = 3
HELM = 0.02
SHIFT = 6.0
MESH = pl.DeviceIdType.MESH

ORDER = (1, 5, 7, 0, 2, 4, 6, 9, 8, 10, 11, 12, 13, 3)
V, CY, RHO, U, W, CX, CZ, A22, A11, A33, A12, A13, A23, TH = range(14)
HALF = 7
THIRD = (2, 1)


def kernel(nx, ny, mom, theta, cour, dens, diag, cross, mom_out, th_out, p_out,
           cells, rows, edges, packed, beside, corner, first, second, coef,
           kry, rhs_rows, rhs_packed, rhs_beside, rhs_corner,
           part, part_x, sum_x, part_y, in_sem, send_sem, recv_sem):
    gx = lax.axis_index("gx")
    gy = lax.axis_index("gy")
    nz = rows.shape[2]
    ny_dev = 8
    plane = nz * ny_dev

    def device(dx, dy):
        return {"gx": lax.rem(gx + dx + nx, nx), "gy": gy + dy}

    barrier = pltpu.get_barrier_semaphore()
    peers = [(lax.rem(gx + d, nx), gy) for d in range(1, nx)]
    peers += [(gx, lax.rem(gy + d, ny)) for d in range(1, ny)]
    peers += [(lax.rem(gx + a, nx), lax.rem(gy + b, ny)) for a in (1, nx - 1) for b in (1, ny - 1)]
    for a, b in peers:
        pl.semaphore_signal(barrier, inc=1, device_id={"gx": a, "gy": b}, device_id_type=MESH)

    loads = []
    place = 0
    for n, ref in enumerate((mom, theta, cour, dens, diag, cross)):
        size = ref.shape[0]
        loads.append(pltpu.make_async_copy(ref, cells.at[pl.ds(place, size)], in_sem.at[n]))
        place += size
    for n in (0, 2, 3, 1, 4, 5):
        loads[n].start()

    def clear(lo):
        rows[lo:lo + 3] = jnp.zeros((3,) + rows.shape[1:], jnp.float32)
        edges[lo:lo + 3] = jnp.zeros((3,) + edges.shape[1:], jnp.float32)
        for i in range(lo, lo + 3):
            rows[i, RHO] = jnp.ones(rows.shape[2:], jnp.float32)
            edges[i, RHO] = jnp.ones(rows.shape[2:], jnp.float32)
        rhs_rows[lo:lo + 3] = jnp.zeros((3,) + rhs_rows.shape[1:], jnp.float32)

    pl.when(gy == 0)(lambda: clear(0))
    pl.when(gy == ny - 1)(lambda: clear(11))

    lane = lax.broadcasted_iota(jnp.int32, (nz, 128), 1)
    level = lax.broadcasted_iota(jnp.int32, (nz, 128), 0)
    slot = lane // 8
    from_left = lax.rem(lane, 8) < 4
    wide_level = lax.broadcasted_iota(jnp.int32, (nz, 256), 0)
    last = wide_level == nz - 1
    ground = wide_level == 0

    def xm(a):
        return pltpu.roll(a, 1, 1)

    def xp(a):
        return pltpu.roll(a, 255, 1)

    def zp(a):
        return jnp.where(last, 0.0, pltpu.roll(a, nz - 1, 0))

    def zm(a):
        return jnp.where(ground, 0.0, pltpu.roll(a, 1, 0))

    def grouped(lo, hi, size, body, stride=None):
        stride = size if stride is None else stride
        count = (hi - lo) // stride
        if count == 1:
            body(lo)
            return

        def step(n, _):
            body(lo + n * stride)
            return 0
        lax.fori_loop(0, count, step, 0)

    def load_half(b):
        def some(j0):
            for j in (j0, j0 + 1):
                for f in range(b * HALF, b * HALF + HALF):
                    value = cells[pl.ds(ORDER[f] * plane + j, nz, stride=ny_dev), :]
                    if f == CY:
                        value = jnp.where(gy * ny_dev + j == 0, 0.0, value)
                    if f == CZ:
                        value = jnp.where(level == 0, 0.0, value)
                    rows[3 + j, f] = value
        grouped(0, ny_dev, 2, some)

    def pack_half(b):
        def one(t, _):
            acc = jnp.zeros((nz, 128), jnp.float32)
            for side in range(2):
                for fi in range(HALF):
                    p = 64 * side + 8 * fi
                    moved = pltpu.roll(rows[3 + 2 * t + side, b * HALF + fi], (p + 4) % 128, 1)
                    acc = jnp.where(slot == p // 8, moved, acc)
            for fi in range(THIRD[b]):
                p = 56 + 64 * fi
                moved = pltpu.roll(rows[5 + 3 * (t // 2), b * HALF + fi], (p + 4) % 128, 1)
                acc = jnp.where(slot == p // 8, moved, acc)
            packed[b, t] = acc
            return 0
        lax.fori_loop(0, ny_dev // 2, one, 0)

    def spread(b, tile, side, row):
        for fi in range(HALF):
            p = 64 * side + 8 * fi
            edges[row, b * HALF + fi] = pltpu.roll(tile, (128 - (p + 4)) % 128, 1)

    def unpack_own(b):
        def one(t, _):
            tile = jnp.where(from_left, beside[b, 0, t], beside[b, 1, t])
            for side in range(2):
                spread(b, tile, side, 3 + 2 * t + side)
            return 0
        lax.fori_loop(0, ny_dev // 2, one, 0)

    def unpack_halo(b):
        def one(side, near, third):
            tile = jnp.where(from_left, corner[b, side, 0], corner[b, side, 1])
            spread(b, tile, 0, near)
            spread(b, tile, 1, near + 1)
            for fi in range(THIRD[b]):
                edges[third, b * HALF + fi] = pltpu.roll(tile, (128 - (60 + 64 * fi)) % 128, 1)

        pl.when(gy > 0)(lambda: one(0, 1, 0))
        pl.when(gy < ny - 1)(lambda: one(1, 11, 13))

    def remote(src, dst, k, dx, dy):
        return pltpu.make_async_remote_copy(
            src_ref=src, dst_ref=dst, send_sem=send_sem.at[k], recv_sem=recv_sem.at[k],
            device_id=device(dx, dy), device_id_type=MESH)

    def group(entries, base):
        by = {1: [], -1: [], 0: []}
        for n, (dx, dy, src, dst) in enumerate(entries):
            by[dy].append((src, dst, base + n, dx, dy))
        return by

    def each(by, action, sign, order=(0, 1, -1)):
        for dy in order:
            def run(dy=dy):
                for item in by[dy]:
                    action(remote(*item))
            if dy == 0:
                run()
            elif dy * sign == 1:
                pl.when(gy < ny - 1)(run)
            else:
                pl.when(gy > 0)(run)

    def start(by):
        each(by, lambda c: c.start(), 1)

    def wait_beside(by):
        each(by, lambda c: c.wait_recv(), -1, (0,))

    def wait_halo(by):
        each(by, lambda c: c.wait_recv(), -1, (1, -1))

    def wait_send(by):
        each(by, lambda c: c.wait_send(), 1)

    def half_entries(b):
        fs = pl.ds(b * HALF, HALF)
        ft = pl.ds(b * HALF, THIRD[b])
        return [
            (0, 1, rows.at[pl.ds(9, 2), fs], rows.at[pl.ds(1, 2), fs]),
            (0, 1, rows.at[pl.ds(8, 1), ft], rows.at[pl.ds(0, 1), ft]),
            (0, -1, rows.at[pl.ds(3, 2), fs], rows.at[pl.ds(11, 2), fs]),
            (0, -1, rows.at[pl.ds(5, 1), ft], rows.at[pl.ds(13, 1), ft]),
            (1, 0, packed.at[b], beside.at[b, 0]),
            (-1, 0, packed.at[b], beside.at[b, 1]),
            (1, 1, packed.at[b, 3], corner.at[b, 0, 0]),
            (-1, 1, packed.at[b, 3], corner.at[b, 0, 1]),
            (1, -1, packed.at[b, 0], corner.at[b, 1, 0]),
            (-1, -1, packed.at[b, 0], corner.at[b, 1, 1]),
        ]

    half_a = group(half_entries(0), 0)
    half_b = group(half_entries(1), 10)
    half_r = group([
        (0, 1, rhs_rows.at[pl.ds(8, 3)], rhs_rows.at[pl.ds(0, 3)]),
        (0, -1, rhs_rows.at[pl.ds(3, 3)], rhs_rows.at[pl.ds(11, 3)]),
        (1, 0, rhs_packed, rhs_beside.at[0]),
        (-1, 0, rhs_packed, rhs_beside.at[1]),
        (1, 1, rhs_packed, rhs_corner.at[0, 0]),
        (-1, 1, rhs_packed, rhs_corner.at[0, 1]),
        (1, -1, rhs_packed, rhs_corner.at[1, 0]),
        (-1, -1, rhs_packed, rhs_corner.at[1, 1]),
    ], 20)

    for n in (0, 2, 3):
        loads[n].wait()
    load_half(0)
    pack_half(0)
    pl.semaphore_wait(barrier, len(peers))
    start(half_a)
    for n in (1, 4, 5):
        loads[n].wait()
    load_half(1)
    pack_half(1)
    start(half_b)

    def wide(r, f):
        return jnp.concatenate([rows[r, f], edges[r, f]], axis=1)

    def upwind(fields, lo, hi, size, stride=None):
        def some(r0):
            span = range(size)
            cys = [wide(r0 + i, CY) for i in range(size + 1)]
            cys = [(jnp.maximum(c, 0.0), jnp.minimum(c, 0.0)) for c in cys]
            psi = {f: [wide(r0 + i - 1, f) for i in range(size + 2)] for _, f in fields}
            for i in span:
                r = r0 + i
                cx, cz = wide(r, CX), wide(r, CZ)
                inv = 1.0 / wide(r, RHO)
                cx_p, cx_n = jnp.maximum(cx, 0.0), jnp.minimum(cx, 0.0)
                cz_p, cz_n = jnp.maximum(cz, 0.0), jnp.minimum(cz, 0.0)
                for n, f in fields:
                    below, here, above = psi[f][i:i + 3]
                    fx = cx_p * xm(here) + cx_n * here
                    fz = cz_p * zm(here) + cz_n * here
                    fy = cys[i][0] * below + cys[i][1] * here
                    fu = cys[i + 1][0] * here + cys[i + 1][1] * above
                    total = xp(fx) - fx + fu - fy + zp(fz) - fz
                    first[r, n] = here - total * inv
        grouped(lo, hi, size, some, stride)

    def face(c, a, b):
        return 0.5 * jnp.abs(c) - c * c / (a + b)

    def antidiffuse(fields, lo, hi, size, stride=None):
        def some(r0):
            rhos = [wide(r0 + i - 1, RHO) for i in range(size + 2)]
            kys = [face(wide(r0 + i, CY), rhos[i], rhos[i + 1]) for i in range(size + 1)]
            for i in range(size):
                r = r0 + i
                rho = rhos[i + 1]
                inv = 1.0 / rho
                kx = face(wide(r, CX), xm(rho), rho)
                kz = face(wide(r, CZ), zm(rho), rho)
                for n in fields:
                    here = first[r, n]
                    ax = kx * (here - xm(here))
                    az = kz * (here - zm(here))
                    ay = kys[i] * (here - first[r - 1, n])
                    au = kys[i + 1] * (first[r + 1, n] - here)
                    total = xp(ax) - ax + au - ay + zp(az) - az
                    second[r, n] = here - total * inv
        grouped(lo, hi, size, some, stride)

    wind = ((0, U), (1, V), (2, W))
    wait_beside(half_a)
    unpack_own(0)
    upwind(wind, 4, 10, 3)
    antidiffuse((0, 1, 2), 5, 9, 2)
    wait_halo(half_a)
    unpack_halo(0)
    upwind(wind, 1, 19, 3, 9)
    antidiffuse((0, 1, 2), 2, 16, 3, 7)

    acc = jnp.zeros((nz, 128), jnp.float32)
    for j in range(ny_dev):
        r = 3 + j
        u, w = second[r, 0], second[r, 2]
        value = (0.5 * (xp(u) - xm(u)) + 0.5 * (second[r + 1, 1] - second[r - 1, 1])
                 + 0.5 * (zp(w) - zm(w)))[:, :128]
        rhs_rows[r] = value
        acc = jnp.where(slot == j, pltpu.roll(value, 8 * j + 4, 1), acc)
    rhs_packed[...] = acc
    start(half_r)

    wait_beside(half_b)
    unpack_own(1)
    wait_halo(half_b)
    unpack_halo(1)

    def make_coef(r0):
        size = 4
        a22s = [wide(r0 + i - 1, A22) for i in range(size + 2)]
        wys = []
        for i in range(size + 1):
            at = gy * ny_dev + r0 + i - 3
            wys.append(jnp.where((at > 0) & (at < ny * ny_dev), 0.5 * (a22s[i] + a22s[i + 1]), 0.0))
        for i in range(size):
            r = r0 + i
            a11, a33 = wide(r, A11), wide(r, A33)
            wxl = 0.5 * (xm(a11) + a11)
            wx = xp(wxl)
            wyl, wy = wys[i], wys[i + 1]
            wzl = jnp.where(ground, 0.0, 0.5 * (zm(a33) + a33))
            wz = zp(wzl)
            coef[r, 0] = wx
            coef[r, 1] = wxl
            coef[r, 2] = wy
            coef[r, 3] = wyl
            coef[r, 4] = wz
            coef[r, 5] = wzl
            coef[r, 6] = (SHIFT - HELM) - (wx + wxl + wy + wyl + wz + wzl)
            coef[r, 7] = 0.25 * wide(r, A12)
            coef[r, 8] = 0.25 * wide(r, A13)
            coef[r, 9] = 0.25 * wide(r, A23)

    grouped(1, 13, 4, make_coef)

    def spread_rhs(j, tile, row):
        edge = pltpu.roll(tile, 128 - (8 * j + 4), 1)
        kry[0, row] = jnp.concatenate([rhs_rows[row], edge], axis=1)

    def halo_rhs(side, js, lo, inside):
        @pl.when(inside)
        def _():
            tile = jnp.where(from_left, rhs_corner[side, 0], rhs_corner[side, 1])
            for n, j in enumerate(js):
                spread_rhs(j, tile, lo + n)

        @pl.when(jnp.logical_not(inside))
        def _():
            for n in range(3):
                kry[0, lo + n] = jnp.zeros((nz, 256), jnp.float32)

    def operate(n, r0, size):
        ps = [kry[n, r0 + i - 1] for i in range(size + 2)]
        sides = [(xp(p), xm(p)) for p in ps]
        dxs = [right - left for right, left in sides]
        out = []
        for i in range(size):
            r = r0 + i
            down, p, up = ps[i:i + 3]
            right, left = sides[i + 1]
            dx, dy = dxs[i + 1], up - down
            out.append(
                coef[r, 0] * right + coef[r, 1] * left + coef[r, 2] * up + coef[r, 3] * down
                + coef[r, 4] * zp(p) + coef[r, 5] * zm(p) + coef[r, 6] * p
                + coef[r, 7] * (dxs[i + 2] - dxs[i])
                + coef[r, 8] * (zp(dx) - zm(dx)) + coef[r, 9] * (zp(dy) - zm(dy)))
        return out

    def lift(n, lo, hi, size, stride=None):
        def some(r0):
            for i, value in enumerate(operate(n, r0, size)):
                kry[n + 1, r0 + i] = value
        grouped(lo, hi, size, some, stride)

    pairs = [(a, b) for a in range(ITERS + 1) for b in range(a, ITERS + 1)]

    def gram(acc, r0, size):
        tops = operate(ITERS - 1, r0, size)
        acc = list(acc)
        for i in range(size):
            vecs = [kry[n, r0 + i][:, :128] for n in range(ITERS)] + [tops[i][:, :128]]
            for n, (a, b) in enumerate(pairs):
                prod = vecs[a] * vecs[b]
                acc[n] = acc[n] + (prod[:8] + prod[8:])
        return tuple(acc)

    wait_beside(half_r)
    tile = jnp.where(from_left, rhs_beside[0], rhs_beside[1])
    for j in range(ny_dev):
        spread_rhs(j, tile, 3 + j)
    lift(0, 4, 10, 3)
    lift(1, 5, 9, 4)
    sums = gram(tuple(jnp.zeros((8, 128), jnp.float32) for _ in pairs), 6, 2)
    wait_halo(half_r)
    halo_rhs(0, (5, 6, 7), 0, gy > 0)
    halo_rhs(1, (0, 1, 2), 11, gy < ny - 1)
    lift(0, 1, 19, 3, 9)
    lift(1, 2, 16, 3, 7)
    sums = lax.fori_loop(0, 2, lambda n, acc: gram(acc, 3 + 5 * n, 3), sums)
    spot = lax.broadcasted_iota(jnp.int32, (16, 128), 0)
    tile = jnp.zeros((16, 128), jnp.float32)
    for n, s in enumerate(sums):
        tile = jnp.where(spot == n, jnp.sum(s, axis=0, keepdims=True), tile)
    part[...] = tile

    def x_copy(d):
        k = 28 + d - 1
        return pltpu.make_async_remote_copy(
            src_ref=part, dst_ref=part_x.at[d - 1], send_sem=send_sem.at[k], recv_sem=recv_sem.at[k],
            device_id={"gx": lax.rem(gx + d, nx), "gy": gy}, device_id_type=MESH)

    def y_copy(d):
        k = 28 + nx - 1 + d - 1
        return pltpu.make_async_remote_copy(
            src_ref=sum_x, dst_ref=part_y.at[d - 1], send_sem=send_sem.at[k], recv_sem=recv_sem.at[k],
            device_id={"gx": gx, "gy": lax.rem(gy + d, ny)}, device_id_type=MESH)

    for d in range(1, nx):
        x_copy(d).start()
    upwind(((3, TH),), 2, 12, 5)
    for d in range(1, nx):
        x_copy(d).wait_recv()
    tile = part[...]
    for d in range(1, nx):
        tile = tile + part_x[d - 1]
    sum_x[...] = tile
    for d in range(1, ny):
        y_copy(d).start()
    antidiffuse((3,), 3, 11, 4)

    def store(ref, base, j, value):
        ref[pl.ds(base + j, nz, stride=ny_dev), :] = value

    for j in range(ny_dev):
        store(th_out, 0, j, second[3 + j, 3][:, :128])
    for d in range(1, ny):
        y_copy(d).wait_recv()
    tile = sum_x[...]
    for d in range(1, ny):
        tile = tile + part_y[d - 1]
    total = jnp.sum(tile, axis=1, keepdims=True)
    gmat = {}
    for n, (a, b) in enumerate(pairs):
        gmat[a, b] = gmat[b, a] = total[n:n + 1, :]

    def dot(a, b):
        terms = [x * y for x, y in zip(a, b) if x is not None and y is not None]
        return functools.reduce(lambda s, t: s + t, terms)

    def minus(a, s, b):
        out = []
        for x, y in zip(a, b):
            if y is None:
                out.append(x)
            else:
                out.append(-(s * y) if x is None else x - s * y)
        return out

    def image(a):
        out = [None if x is None else -SHIFT * x for x in a]
        for n in range(ITERS):
            if a[n] is not None:
                out[n + 1] = a[n] if out[n + 1] is None else out[n + 1] + a[n]
        return out

    one = jnp.ones((1, 1), jnp.float32)
    resid = [one] + [None] * ITERS
    dirs, images, duals, norms = [resid], [image(resid)], [], []
    press = [None] * (ITERS + 1)
    for step in range(ITERS):
        q = images[step]
        dual = [dot([gmat[a, b] for b in range(ITERS + 1)], q) for a in range(ITERS + 1)]
        duals.append(dual)
        norms.append(dot(q, dual))
        beta = dot(resid, dual) / norms[step]
        press = minus(press, -beta, dirs[step])
        if step + 1 < ITERS:
            resid = minus(resid, beta, q)
            lifted = image(resid)
            new_dir, new_img = resid, lifted
            for back in range(step + 1):
                alpha = dot(lifted, duals[back]) / norms[back]
                new_dir = minus(new_dir, alpha, dirs[back])
                new_img = minus(new_img, alpha, images[back])
            dirs.append(new_dir)
            images.append(new_img)
    c0, c1, c2 = [jnp.broadcast_to(c, (nz, 256)) for c in press[:ITERS]]

    def pressure(r):
        return c0 * kry[0, r] + c1 * kry[1, r] + c2 * kry[2, r]

    def finish(j0):
        size = 4
        ps = [pressure(3 + j0 + i - 1) for i in range(size + 2)]
        for i in range(size):
            j = j0 + i
            r = 3 + j
            down, here, up = ps[i:i + 3]
            store(p_out, 0, j, here[:, :128])
            store(mom_out, 0, j, (second[r, 0] - 0.5 * (xp(here) - xm(here)))[:, :128])
            store(mom_out, plane, j, (second[r, 1] - 0.5 * (up - down))[:, :128])
            store(mom_out, 2 * plane, j, (second[r, 2] - 0.5 * (zp(here) - zm(here)))[:, :128])

    grouped(0, ny_dev, 4, finish)

    wait_send(half_a)
    wait_send(half_b)
    wait_send(half_r)
    for d in range(1, nx):
        x_copy(d).wait_send()
    for d in range(1, ny):
        y_copy(d).wait_send()


def put_out(mom, th, press, mom_out, th_out, p_out, sem):
    pairs = ((mom, mom_out), (th, th_out), (press, p_out))
    copies = [pltpu.make_async_copy(a, b, sem.at[n]) for n, (a, b) in enumerate(pairs)]
    for copy in copies:
        copy.start()
    for copy in copies:
        copy.wait()


def solution(mesh):
    nx, ny = mesh.shape["gx"], mesh.shape["gy"]

    def local(momenta, theta, courant, density, metric_diag, metric_cross):
        nz, ny_dev, nx_dev = density.shape
        args = (momenta, theta, courant, density, metric_diag, metric_cross)
        flat = [pltpu.with_memory_space_constraint(a.reshape(-1, nx_dev), pltpu.HBM) for a in args]
        plane = nz * ny_dev
        f32 = jnp.float32
        n_ext = ny_dev + 6
        n_sem = 28 + nx - 1 + ny - 1
        shape = jax.ShapeDtypeStruct
        vmem = pltpu.VMEM
        mom, th, press = pl.pallas_call(
            functools.partial(kernel, nx, ny),
            out_shape=(shape((3 * plane, nx_dev), f32), shape((plane, nx_dev), f32),
                       shape((plane, nx_dev), f32)),
            in_specs=[pl.BlockSpec(memory_space=pltpu.HBM)] * 6,
            out_specs=[pl.BlockSpec(memory_space=pltpu.VMEM)] * 3,
            scratch_shapes=[
                vmem((14 * plane, nx_dev), f32),
                vmem((n_ext, 14, nz, nx_dev), f32),
                vmem((n_ext, 14, nz, nx_dev), f32),
                vmem((2, 4, nz, nx_dev), f32),
                vmem((2, 2, 4, nz, nx_dev), f32),
                vmem((2, 2, 2, nz, nx_dev), f32),
                vmem((n_ext, 4, nz, 2 * nx_dev), f32),
                vmem((n_ext, 4, nz, 2 * nx_dev), f32),
                vmem((n_ext, 10, nz, 2 * nx_dev), f32),
                vmem((3, n_ext, nz, 2 * nx_dev), f32),
                vmem((n_ext, nz, nx_dev), f32),
                vmem((nz, nx_dev), f32),
                vmem((2, nz, nx_dev), f32),
                vmem((2, 2, nz, nx_dev), f32),
                vmem((16, 128), f32),
                vmem((nx - 1, 16, 128), f32),
                vmem((16, 128), f32),
                vmem((ny - 1, 16, 128), f32),
                pltpu.SemaphoreType.DMA((6,)),
                pltpu.SemaphoreType.DMA((n_sem,)),
                pltpu.SemaphoreType.DMA((n_sem,)),
            ],
            compiler_params=pltpu.CompilerParams(
                collective_id=0, has_side_effects=True, vmem_limit_bytes=40 * 1024 * 1024),
        )(*flat)
        mom, th, press = pl.pallas_call(
            put_out,
            out_shape=[shape(a.shape, f32) for a in (mom, th, press)],
            in_specs=[pl.BlockSpec(memory_space=pl.ANY)] * 3,
            out_specs=[pl.BlockSpec(memory_space=pltpu.HBM)] * 3,
            scratch_shapes=[pltpu.SemaphoreType.DMA((3,))],
        )(mom, th, press)
        return mom.reshape(momenta.shape), th.reshape(theta.shape), press.reshape(theta.shape)

    placed = (
        P(None, None, "gy", "gx"),
        P(None, "gy", "gx"),
        P(None, None, "gy", "gx"),
        P(None, "gy", "gx"),
        P(None, None, "gy", "gx"),
        P(None, None, "gy", "gx"),
    )
    return jax.shard_map(
        local,
        mesh=mesh,
        in_specs=placed,
        out_specs=(P(None, None, "gy", "gx"), P(None, "gy", "gx"), P(None, "gy", "gx")),
        check_vma=False,
    )
```

```python
import functools

import jax
import jax.numpy as jnp
from jax import lax
from jax.experimental import pallas as pl
from jax.experimental.pallas import tpu as pltpu
from jax.sharding import PartitionSpec as P

ITERS = 3
HELM = 0.02
SHIFT = 6.0
MESH = pl.DeviceIdType.MESH

ORDER = (1, 5, 7, 0, 2, 4, 6, 9, 8, 10, 11, 12, 13, 3)
V, CY, RHO, U, W, CX, CZ, A22, A11, A33, A12, A13, A23, TH = range(14)
HALF = 7
THIRD = (2, 1)


def kernel(nx, ny, mom, theta, cour, dens, diag, cross, mom_out, th_out, p_out,
           cells, rows, edges, packed, beside, corner, first, second, coef,
           kry, rhs_rows, rhs_packed, rhs_beside, rhs_corner,
           part, parts, in_sem, send_sem, recv_sem):
    gx = lax.axis_index("gx")
    gy = lax.axis_index("gy")
    nz = rows.shape[2]
    ny_dev = 8
    plane = nz * ny_dev

    def device(dx, dy):
        return {"gx": lax.rem(gx + dx + nx, nx), "gy": gy + dy}

    barrier = pltpu.get_barrier_semaphore()
    count = nx * ny
    me = gx * ny + gy

    def peer(d):
        other = lax.rem(me + d, count)
        return {"gx": other // ny, "gy": lax.rem(other, ny)}

    def every_peer(body):
        if count <= 64:
            for d in range(1, count):
                body(d)
        else:
            def step(d, _):
                body(d)
                return 0
            lax.fori_loop(1, count, step, 0)

    every_peer(lambda d: pl.semaphore_signal(barrier, inc=1, device_id=peer(d), device_id_type=MESH))

    loads = []
    place = 0
    for n, ref in enumerate((mom, theta, cour, dens, diag, cross)):
        size = ref.shape[0]
        loads.append(pltpu.make_async_copy(ref, cells.at[pl.ds(place, size)], in_sem.at[n]))
        place += size
    for n in (0, 2, 3, 1, 4, 5):
        loads[n].start()

    def clear(lo):
        rows[lo:lo + 3] = jnp.zeros((3,) + rows.shape[1:], jnp.float32)
        edges[lo:lo + 3] = jnp.zeros((3,) + edges.shape[1:], jnp.float32)
        for i in range(lo, lo + 3):
            rows[i, RHO] = jnp.ones(rows.shape[2:], jnp.float32)
            edges[i, RHO] = jnp.ones(rows.shape[2:], jnp.float32)
        rhs_rows[lo:lo + 3] = jnp.zeros((3,) + rhs_rows.shape[1:], jnp.float32)

    pl.when(gy == 0)(lambda: clear(0))
    pl.when(gy == ny - 1)(lambda: clear(11))

    lane = lax.broadcasted_iota(jnp.int32, (nz, 128), 1)
    level = lax.broadcasted_iota(jnp.int32, (nz, 128), 0)
    slot = lane // 8
    from_left = lax.rem(lane, 8) < 4
    wide_level = lax.broadcasted_iota(jnp.int32, (nz, 256), 0)
    last = wide_level == nz - 1
    ground = wide_level == 0

    def xm(a):
        return pltpu.roll(a, 1, 1)

    def xp(a):
        return pltpu.roll(a, 255, 1)

    def zp(a):
        return jnp.where(last, 0.0, pltpu.roll(a, nz - 1, 0))

    def zm(a):
        return jnp.where(ground, 0.0, pltpu.roll(a, 1, 0))

    def grouped(lo, hi, size, body, stride=None):
        stride = size if stride is None else stride
        count = (hi - lo) // stride
        if count == 1:
            body(lo)
            return

        def step(n, _):
            body(lo + n * stride)
            return 0
        lax.fori_loop(0, count, step, 0)

    def load_half(b):
        def some(j0):
            for j in (j0, j0 + 1):
                for f in range(b * HALF, b * HALF + HALF):
                    value = cells[pl.ds(ORDER[f] * plane + j, nz, stride=ny_dev), :]
                    if f == CY:
                        value = jnp.where(gy * ny_dev + j == 0, 0.0, value)
                    if f == CZ:
                        value = jnp.where(level == 0, 0.0, value)
                    rows[3 + j, f] = value
        grouped(0, ny_dev, 2, some)

    def pack_half(b):
        def one(t, _):
            acc = jnp.zeros((nz, 128), jnp.float32)
            for side in range(2):
                for fi in range(HALF):
                    p = 64 * side + 8 * fi
                    moved = pltpu.roll(rows[3 + 2 * t + side, b * HALF + fi], (p + 4) % 128, 1)
                    acc = jnp.where(slot == p // 8, moved, acc)
            for fi in range(THIRD[b]):
                p = 56 + 64 * fi
                moved = pltpu.roll(rows[5 + 3 * (t // 2), b * HALF + fi], (p + 4) % 128, 1)
                acc = jnp.where(slot == p // 8, moved, acc)
            packed[b, t] = acc
            return 0
        lax.fori_loop(0, ny_dev // 2, one, 0)

    def spread(b, tile, side, row):
        for fi in range(HALF):
            p = 64 * side + 8 * fi
            edges[row, b * HALF + fi] = pltpu.roll(tile, (128 - (p + 4)) % 128, 1)

    def unpack_own(b):
        def one(t, _):
            tile = jnp.where(from_left, beside[b, 0, t], beside[b, 1, t])
            for side in range(2):
                spread(b, tile, side, 3 + 2 * t + side)
            return 0
        lax.fori_loop(0, ny_dev // 2, one, 0)

    def unpack_halo(b):
        def one(side, near, third):
            tile = jnp.where(from_left, corner[b, side, 0], corner[b, side, 1])
            spread(b, tile, 0, near)
            spread(b, tile, 1, near + 1)
            for fi in range(THIRD[b]):
                edges[third, b * HALF + fi] = pltpu.roll(tile, (128 - (60 + 64 * fi)) % 128, 1)

        pl.when(gy > 0)(lambda: one(0, 1, 0))
        pl.when(gy < ny - 1)(lambda: one(1, 11, 13))

    def remote(src, dst, k, dx, dy):
        return pltpu.make_async_remote_copy(
            src_ref=src, dst_ref=dst, send_sem=send_sem.at[k], recv_sem=recv_sem.at[k],
            device_id=device(dx, dy), device_id_type=MESH)

    def group(entries, base):
        by = {1: [], -1: [], 0: []}
        for n, (dx, dy, src, dst) in enumerate(entries):
            by[dy].append((src, dst, base + n, dx, dy))
        return by

    def each(by, action, sign, order=(0, 1, -1)):
        for dy in order:
            def run(dy=dy):
                for item in by[dy]:
                    action(remote(*item))
            if dy == 0:
                run()
            elif dy * sign == 1:
                pl.when(gy < ny - 1)(run)
            else:
                pl.when(gy > 0)(run)

    def start(by):
        each(by, lambda c: c.start(), 1)

    def wait_beside(by):
        each(by, lambda c: c.wait_recv(), -1, (0,))

    def wait_halo(by):
        each(by, lambda c: c.wait_recv(), -1, (1, -1))

    def wait_send(by):
        each(by, lambda c: c.wait_send(), 1)

    def half_entries(b):
        fs = pl.ds(b * HALF, HALF)
        ft = pl.ds(b * HALF, THIRD[b])
        return [
            (0, 1, rows.at[pl.ds(9, 2), fs], rows.at[pl.ds(1, 2), fs]),
            (0, 1, rows.at[pl.ds(8, 1), ft], rows.at[pl.ds(0, 1), ft]),
            (0, -1, rows.at[pl.ds(3, 2), fs], rows.at[pl.ds(11, 2), fs]),
            (0, -1, rows.at[pl.ds(5, 1), ft], rows.at[pl.ds(13, 1), ft]),
            (1, 0, packed.at[b], beside.at[b, 0]),
            (-1, 0, packed.at[b], beside.at[b, 1]),
            (1, 1, packed.at[b, 3], corner.at[b, 0, 0]),
            (-1, 1, packed.at[b, 3], corner.at[b, 0, 1]),
            (1, -1, packed.at[b, 0], corner.at[b, 1, 0]),
            (-1, -1, packed.at[b, 0], corner.at[b, 1, 1]),
        ]

    half_a = group(half_entries(0), 0)
    half_b = group(half_entries(1), 10)
    half_r = group([
        (0, 1, rhs_rows.at[pl.ds(8, 3)], rhs_rows.at[pl.ds(0, 3)]),
        (0, -1, rhs_rows.at[pl.ds(3, 3)], rhs_rows.at[pl.ds(11, 3)]),
        (1, 0, rhs_packed, rhs_beside.at[0]),
        (-1, 0, rhs_packed, rhs_beside.at[1]),
        (1, 1, rhs_packed, rhs_corner.at[0, 0]),
        (-1, 1, rhs_packed, rhs_corner.at[0, 1]),
        (1, -1, rhs_packed, rhs_corner.at[1, 0]),
        (-1, -1, rhs_packed, rhs_corner.at[1, 1]),
    ], 20)

    for n in (0, 2, 3):
        loads[n].wait()
    load_half(0)
    pack_half(0)
    pl.semaphore_wait(barrier, count - 1)
    start(half_a)
    for n in (1, 4, 5):
        loads[n].wait()
    load_half(1)
    pack_half(1)
    start(half_b)

    def wide(r, f):
        return jnp.concatenate([rows[r, f], edges[r, f]], axis=1)

    def upwind(fields, lo, hi, size, stride=None):
        def some(r0):
            span = range(size)
            for i in span:
                r = r0 + i
                cx, cz = wide(r, CX), wide(r, CZ)
                inv = 1.0 / wide(r, RHO)
                cx_p, cx_n = jnp.maximum(cx, 0.0), jnp.minimum(cx, 0.0)
                cz_p, cz_n = jnp.maximum(cz, 0.0), jnp.minimum(cz, 0.0)
                cy, cu = wide(r, CY), wide(r + 1, CY)
                cy_p, cy_n = jnp.maximum(cy, 0.0), jnp.minimum(cy, 0.0)
                cu_p, cu_n = jnp.maximum(cu, 0.0), jnp.minimum(cu, 0.0)
                for n, f in fields:
                    here = wide(r, f)
                    fx = cx_p * xm(here) + cx_n * here
                    fz = cz_p * zm(here) + cz_n * here
                    fy = cy_p * wide(r - 1, f) + cy_n * here
                    fu = cu_p * here + cu_n * wide(r + 1, f)
                    total = xp(fx) - fx + fu - fy + zp(fz) - fz
                    first[r, n] = here - total * inv
        grouped(lo, hi, size, some, stride)

    def face(c, a, b):
        return 0.5 * jnp.abs(c) - c * c / (a + b)

    def antidiffuse(fields, lo, hi, size, stride=None):
        def some(r0):
            ku = face(wide(r0, CY), wide(r0 - 1, RHO), wide(r0, RHO))
            for i in range(size):
                r = r0 + i
                rho = wide(r, RHO)
                inv = 1.0 / rho
                ky, ku = ku, face(wide(r + 1, CY), rho, wide(r + 1, RHO))
                kx = face(wide(r, CX), xm(rho), rho)
                kz = face(wide(r, CZ), zm(rho), rho)
                for n in fields:
                    here = first[r, n]
                    ax = kx * (here - xm(here))
                    az = kz * (here - zm(here))
                    ay = ky * (here - first[r - 1, n])
                    au = ku * (first[r + 1, n] - here)
                    total = xp(ax) - ax + au - ay + zp(az) - az
                    second[r, n] = here - total * inv
        grouped(lo, hi, size, some, stride)

    wind = ((0, U), (1, V), (2, W))
    wait_beside(half_a)
    unpack_own(0)
    upwind(wind, 4, 10, 3)
    antidiffuse((0, 1, 2), 5, 9, 2)
    wait_halo(half_a)
    unpack_halo(0)
    upwind(wind, 1, 19, 3, 9)
    antidiffuse((0, 1, 2), 2, 16, 3, 7)

    acc = jnp.zeros((nz, 128), jnp.float32)
    for j in range(ny_dev):
        r = 3 + j
        u, w = second[r, 0], second[r, 2]
        value = (0.5 * (xp(u) - xm(u)) + 0.5 * (second[r + 1, 1] - second[r - 1, 1])
                 + 0.5 * (zp(w) - zm(w)))[:, :128]
        rhs_rows[r] = value
        acc = jnp.where(slot == j, pltpu.roll(value, 8 * j + 4, 1), acc)
    rhs_packed[...] = acc
    start(half_r)

    wait_beside(half_b)
    unpack_own(1)
    wait_halo(half_b)
    unpack_halo(1)

    def make_coef(r0):
        size = 4
        a22s = [wide(r0 + i - 1, A22) for i in range(size + 2)]
        wys = []
        for i in range(size + 1):
            at = gy * ny_dev + r0 + i - 3
            wys.append(jnp.where((at > 0) & (at < ny * ny_dev), 0.5 * (a22s[i] + a22s[i + 1]), 0.0))
        for i in range(size):
            r = r0 + i
            a11, a33 = wide(r, A11), wide(r, A33)
            wxl = 0.5 * (xm(a11) + a11)
            wx = xp(wxl)
            wyl, wy = wys[i], wys[i + 1]
            wzl = jnp.where(ground, 0.0, 0.5 * (zm(a33) + a33))
            wz = zp(wzl)
            coef[r, 0] = wx
            coef[r, 1] = wxl
            coef[r, 2] = wy
            coef[r, 3] = wyl
            coef[r, 4] = wz
            coef[r, 5] = wzl
            coef[r, 6] = (SHIFT - HELM) - (wx + wxl + wy + wyl + wz + wzl)
            coef[r, 7] = 0.25 * wide(r, A12)
            coef[r, 8] = 0.25 * wide(r, A13)
            coef[r, 9] = 0.25 * wide(r, A23)

    grouped(1, 13, 4, make_coef)

    def spread_rhs(j, tile, row):
        edge = pltpu.roll(tile, 128 - (8 * j + 4), 1)
        kry[0, row] = jnp.concatenate([rhs_rows[row], edge], axis=1)

    def halo_rhs(side, js, lo, inside):
        @pl.when(inside)
        def _():
            tile = jnp.where(from_left, rhs_corner[side, 0], rhs_corner[side, 1])
            for n, j in enumerate(js):
                spread_rhs(j, tile, lo + n)

        @pl.when(jnp.logical_not(inside))
        def _():
            for n in range(3):
                kry[0, lo + n] = jnp.zeros((nz, 256), jnp.float32)

    def operate(n, r0, size):
        def sides(r):
            p = kry[n, r]
            right, left = xp(p), xm(p)
            return right, left, right - left

        here, above = sides(r0), sides(r0 + 1)
        below_dx = sides(r0 - 1)[2]
        out = []
        for i in range(size):
            r = r0 + i
            p, up, down = kry[n, r], kry[n, r + 1], kry[n, r - 1]
            if i > 0:
                below_dx, here, above = here[2], above, sides(r + 1)
            right, left, dx = here
            dy = up - down
            out.append(
                coef[r, 0] * right + coef[r, 1] * left + coef[r, 2] * up + coef[r, 3] * down
                + coef[r, 4] * zp(p) + coef[r, 5] * zm(p) + coef[r, 6] * p
                + coef[r, 7] * (above[2] - below_dx)
                + coef[r, 8] * (zp(dx) - zm(dx)) + coef[r, 9] * (zp(dy) - zm(dy)))
        return out

    def lift(n, lo, hi, size, stride=None):
        def some(r0):
            for i, value in enumerate(operate(n, r0, size)):
                kry[n + 1, r0 + i] = value
        grouped(lo, hi, size, some, stride)

    pairs = [(a, b) for a in range(ITERS + 1) for b in range(a, ITERS + 1)]

    def gram(acc, r0, size):
        tops = operate(ITERS - 1, r0, size)
        acc = list(acc)
        for i in range(size):
            vecs = [kry[n, r0 + i][:, :128] for n in range(ITERS)] + [tops[i][:, :128]]
            for n, (a, b) in enumerate(pairs):
                prod = vecs[a] * vecs[b]
                acc[n] = acc[n] + (prod[:8] + prod[8:])
        return tuple(acc)

    wait_beside(half_r)
    tile = jnp.where(from_left, rhs_beside[0], rhs_beside[1])
    for j in range(ny_dev):
        spread_rhs(j, tile, 3 + j)
    lift(0, 4, 10, 3)
    lift(1, 5, 9, 4)
    sums = gram(tuple(jnp.zeros((8, 128), jnp.float32) for _ in pairs), 6, 2)
    wait_halo(half_r)
    halo_rhs(0, (5, 6, 7), 0, gy > 0)
    halo_rhs(1, (0, 1, 2), 11, gy < ny - 1)
    lift(0, 1, 19, 3, 9)
    lift(1, 2, 16, 3, 7)
    sums = lax.fori_loop(0, 2, lambda n, acc: gram(acc, 3 + 5 * n, 3), sums)
    spot = lax.broadcasted_iota(jnp.int32, (16, 128), 0)
    tile = jnp.zeros((16, 128), jnp.float32)
    for n, s in enumerate(sums):
        tile = jnp.where(spot == n, jnp.sum(s, axis=0, keepdims=True), tile)
    half = lane < 64
    folded = tile + pltpu.roll(tile, 64, 1)
    part[...] = jnp.where(half[:8], folded[:8], folded[8:])

    def part_copy(d):
        return pltpu.make_async_remote_copy(
            src_ref=part, dst_ref=parts.at[d - 1], send_sem=send_sem.at[27 + d],
            recv_sem=recv_sem.at[27 + d], device_id=peer(d), device_id_type=MESH)

    every_peer(lambda d: part_copy(d).start())
    upwind(((3, TH),), 2, 12, 5)
    antidiffuse((3,), 3, 11, 4)

    def store(ref, base, j, value):
        ref[pl.ds(base + j, nz, stride=ny_dev), :] = value

    for j in range(ny_dev):
        store(th_out, 0, j, second[3 + j, 3][:, :128])
    every_peer(lambda d: part_copy(d).wait_recv())
    if count <= 64:
        tile = part[...]
        for d in range(1, count):
            tile = tile + parts[d - 1]
    else:
        tile = lax.fori_loop(1, count, lambda d, acc: acc + parts[d - 1], part[...])
    low = jnp.sum(jnp.where(half[:8], tile, 0.0), axis=1, keepdims=True)
    high = jnp.sum(jnp.where(half[:8], 0.0, tile), axis=1, keepdims=True)
    gmat = {}
    for n, (a, b) in enumerate(pairs):
        gmat[a, b] = gmat[b, a] = low[n:n + 1, :] if n < 8 else high[n - 8:n - 7, :]

    def dot(a, b):
        terms = [x * y for x, y in zip(a, b) if x is not None and y is not None]
        return functools.reduce(lambda s, t: s + t, terms)

    def minus(a, s, b):
        out = []
        for x, y in zip(a, b):
            if y is None:
                out.append(x)
            else:
                out.append(-(s * y) if x is None else x - s * y)
        return out

    def image(a):
        out = [None if x is None else -SHIFT * x for x in a]
        for n in range(ITERS):
            if a[n] is not None:
                out[n + 1] = a[n] if out[n + 1] is None else out[n + 1] + a[n]
        return out

    one = jnp.ones((1, 1), jnp.float32)
    resid = [one] + [None] * ITERS
    dirs, images, duals, norms = [resid], [image(resid)], [], []
    press = [None] * (ITERS + 1)
    for step in range(ITERS):
        q = images[step]
        dual = [dot([gmat[a, b] for b in range(ITERS + 1)], q) for a in range(ITERS + 1)]
        duals.append(dual)
        norms.append(dot(q, dual))
        beta = dot(resid, dual) / norms[step]
        press = minus(press, -beta, dirs[step])
        if step + 1 < ITERS:
            resid = minus(resid, beta, q)
            lifted = image(resid)
            new_dir, new_img = resid, lifted
            for back in range(step + 1):
                alpha = dot(lifted, duals[back]) / norms[back]
                new_dir = minus(new_dir, alpha, dirs[back])
                new_img = minus(new_img, alpha, images[back])
            dirs.append(new_dir)
            images.append(new_img)
    c0, c1, c2 = [jnp.broadcast_to(c, (nz, 256)) for c in press[:ITERS]]

    def pressure(r):
        return c0 * kry[0, r] + c1 * kry[1, r] + c2 * kry[2, r]

    def finish(j0):
        size = 4
        ps = [pressure(3 + j0 + i - 1) for i in range(size + 2)]
        for i in range(size):
            j = j0 + i
            r = 3 + j
            down, here, up = ps[i:i + 3]
            store(p_out, 0, j, here[:, :128])
            store(mom_out, 0, j, (second[r, 0] - 0.5 * (xp(here) - xm(here)))[:, :128])
            store(mom_out, plane, j, (second[r, 1] - 0.5 * (up - down))[:, :128])
            store(mom_out, 2 * plane, j, (second[r, 2] - 0.5 * (zp(here) - zm(here)))[:, :128])

    grouped(0, ny_dev, 4, finish)

    wait_send(half_a)
    wait_send(half_b)
    wait_send(half_r)
    every_peer(lambda d: part_copy(d).wait_send())


def solution(mesh):
    nx, ny = mesh.shape["gx"], mesh.shape["gy"]

    def local(momenta, theta, courant, density, metric_diag, metric_cross):
        nz, ny_dev, nx_dev = density.shape
        args = (momenta, theta, courant, density, metric_diag, metric_cross)
        flat = [pltpu.with_memory_space_constraint(a.reshape(-1, nx_dev), pltpu.HBM) for a in args]
        plane = nz * ny_dev
        f32 = jnp.float32
        n_ext = ny_dev + 6
        n_sem = 28 + nx * ny - 1
        shape = jax.ShapeDtypeStruct
        vmem = pltpu.VMEM
        mom, th, press = pl.pallas_call(
            functools.partial(kernel, nx, ny),
            out_shape=(shape((3 * plane, nx_dev), f32), shape((plane, nx_dev), f32),
                       shape((plane, nx_dev), f32)),
            in_specs=[pl.BlockSpec(memory_space=pltpu.HBM)] * 6,
            out_specs=[pl.BlockSpec(memory_space=pltpu.VMEM)] * 3,
            scratch_shapes=[
                vmem((14 * plane, nx_dev), f32),
                vmem((n_ext, 14, nz, nx_dev), f32),
                vmem((n_ext, 14, nz, nx_dev), f32),
                vmem((2, 4, nz, nx_dev), f32),
                vmem((2, 2, 4, nz, nx_dev), f32),
                vmem((2, 2, 2, nz, nx_dev), f32),
                vmem((n_ext, 4, nz, 2 * nx_dev), f32),
                vmem((n_ext, 4, nz, 2 * nx_dev), f32),
                vmem((n_ext, 10, nz, 2 * nx_dev), f32),
                vmem((3, n_ext, nz, 2 * nx_dev), f32),
                vmem((n_ext, nz, nx_dev), f32),
                vmem((nz, nx_dev), f32),
                vmem((2, nz, nx_dev), f32),
                vmem((2, 2, nz, nx_dev), f32),
                vmem((8, 128), f32),
                vmem((nx * ny - 1, 8, 128), f32),
                pltpu.SemaphoreType.DMA((6,)),
                pltpu.SemaphoreType.DMA((n_sem,)),
                pltpu.SemaphoreType.DMA((n_sem,)),
            ],
            compiler_params=pltpu.CompilerParams(
                collective_id=0, has_side_effects=True, vmem_limit_bytes=40 * 1024 * 1024),
        )(*flat)
        return mom.reshape(momenta.shape), th.reshape(theta.shape), press.reshape(theta.shape)

    placed = (
        P(None, None, "gy", "gx"),
        P(None, "gy", "gx"),
        P(None, None, "gy", "gx"),
        P(None, "gy", "gx"),
        P(None, None, "gy", "gx"),
        P(None, None, "gy", "gx"),
    )
    return jax.shard_map(
        local,
        mesh=mesh,
        in_specs=placed,
        out_specs=(P(None, None, "gy", "gx"), P(None, "gy", "gx"), P(None, "gy", "gx")),
        check_vma=False,
    )
```

```python
import functools

import jax
import jax.numpy as jnp
from jax import lax
from jax.experimental import pallas as pl
from jax.experimental.pallas import tpu as pltpu
from jax.sharding import PartitionSpec as P

ITERS = 3
HELM = 0.02
SHIFT = 6.0
MESH = pl.DeviceIdType.MESH

ORDER = (1, 5, 7, 0, 2, 4, 6, 9, 8, 10, 11, 12, 13, 3)
V, CY, RHO, U, W, CX, CZ, A22, A11, A33, A12, A13, A23, TH = range(14)
HALF = 7
THIRD = (2, 1)


def kernel(nx, ny, mom, theta, cour, dens, diag, cross, mom_out, th_out, p_out,
           cells, rows, edges, packed, beside, corner, first, second, coef,
           kry, rhs_rows, rhs_packed, rhs_beside, rhs_corner,
           part, parts, in_sem, send_sem, recv_sem):
    gx = lax.axis_index("gx")
    gy = lax.axis_index("gy")
    nz = rows.shape[2]
    ny_dev = 8
    plane = nz * ny_dev

    def device(dx, dy):
        return {"gx": lax.rem(gx + dx + nx, nx), "gy": gy + dy}

    barrier = pltpu.get_barrier_semaphore()
    count = nx * ny
    me = gx * ny + gy

    def peer(d):
        other = lax.rem(me + d, count)
        return {"gx": other // ny, "gy": lax.rem(other, ny)}

    def every_peer(body):
        if count <= 64:
            for d in range(1, count):
                body(d)
        else:
            def step(d, _):
                body(d)
                return 0
            lax.fori_loop(1, count, step, 0)

    every_peer(lambda d: pl.semaphore_signal(barrier, inc=1, device_id=peer(d), device_id_type=MESH))

    loads = []
    place = 0
    for n, ref in enumerate((mom, theta, cour, dens, diag, cross)):
        size = ref.shape[0]
        loads.append(pltpu.make_async_copy(ref, cells.at[pl.ds(place, size)], in_sem.at[n]))
        place += size
    for n in (0, 2, 3, 1, 4, 5):
        loads[n].start()

    def clear(lo):
        rows[lo:lo + 3] = jnp.zeros((3,) + rows.shape[1:], jnp.float32)
        edges[lo:lo + 3] = jnp.zeros((3,) + edges.shape[1:], jnp.float32)
        for i in range(lo, lo + 3):
            rows[i, RHO] = jnp.ones(rows.shape[2:], jnp.float32)
            edges[i, RHO] = jnp.ones(rows.shape[2:], jnp.float32)
        rhs_rows[lo:lo + 3] = jnp.zeros((3,) + rhs_rows.shape[1:], jnp.float32)

    pl.when(gy == 0)(lambda: clear(0))
    pl.when(gy == ny - 1)(lambda: clear(11))

    lane = lax.broadcasted_iota(jnp.int32, (nz, 128), 1)
    level = lax.broadcasted_iota(jnp.int32, (nz, 128), 0)
    slot = lane // 8
    from_left = lax.rem(lane, 8) < 4
    wide_level = lax.broadcasted_iota(jnp.int32, (nz, 256), 0)
    last = wide_level == nz - 1
    ground = wide_level == 0

    def xm(a):
        return pltpu.roll(a, 1, 1)

    def xp(a):
        return pltpu.roll(a, 255, 1)

    def zp(a):
        return jnp.where(last, 0.0, pltpu.roll(a, nz - 1, 0))

    def zm(a):
        return jnp.where(ground, 0.0, pltpu.roll(a, 1, 0))

    def grouped(lo, hi, size, body, stride=None):
        stride = size if stride is None else stride
        for r0 in range(lo, lo + (hi - lo) // stride * stride, stride):
            body(r0)

    def load_half(b):
        def some(j0):
            for j in (j0, j0 + 1):
                for f in range(b * HALF, b * HALF + HALF):
                    value = cells[pl.ds(ORDER[f] * plane + j, nz, stride=ny_dev), :]
                    if f == CY:
                        value = jnp.where(gy * ny_dev + j == 0, 0.0, value)
                    if f == CZ:
                        value = jnp.where(level == 0, 0.0, value)
                    rows[3 + j, f] = value
        grouped(0, ny_dev, 2, some)

    def pack_half(b):
        for t in range(ny_dev // 2):
            acc = jnp.zeros((nz, 128), jnp.float32)
            for side in range(2):
                for fi in range(HALF):
                    p = 64 * side + 8 * fi
                    moved = pltpu.roll(rows[3 + 2 * t + side, b * HALF + fi], (p + 4) % 128, 1)
                    acc = jnp.where(slot == p // 8, moved, acc)
            for fi in range(THIRD[b]):
                p = 56 + 64 * fi
                moved = pltpu.roll(rows[5 + 3 * (t // 2), b * HALF + fi], (p + 4) % 128, 1)
                acc = jnp.where(slot == p // 8, moved, acc)
            packed[b, t] = acc

    def spread(b, tile, side, row):
        for fi in range(HALF):
            p = 64 * side + 8 * fi
            edges[row, b * HALF + fi] = pltpu.roll(tile, (128 - (p + 4)) % 128, 1)

    def unpack_own(b):
        for t in range(ny_dev // 2):
            tile = jnp.where(from_left, beside[b, 0, t], beside[b, 1, t])
            for side in range(2):
                spread(b, tile, side, 3 + 2 * t + side)

    def unpack_halo(b):
        def one(side, near, third):
            tile = jnp.where(from_left, corner[b, side, 0], corner[b, side, 1])
            spread(b, tile, 0, near)
            spread(b, tile, 1, near + 1)
            for fi in range(THIRD[b]):
                edges[third, b * HALF + fi] = pltpu.roll(tile, (128 - (60 + 64 * fi)) % 128, 1)

        pl.when(gy > 0)(lambda: one(0, 1, 0))
        pl.when(gy < ny - 1)(lambda: one(1, 11, 13))

    def remote(src, dst, k, dx, dy):
        return pltpu.make_async_remote_copy(
            src_ref=src, dst_ref=dst, send_sem=send_sem.at[k], recv_sem=recv_sem.at[k],
            device_id=device(dx, dy), device_id_type=MESH)

    def group(entries, base):
        by = {1: [], -1: [], 0: []}
        for n, (dx, dy, src, dst) in enumerate(entries):
            by[dy].append((src, dst, base + n, dx, dy))
        return by

    def each(by, action, sign, order=(0, 1, -1)):
        for dy in order:
            def run(dy=dy):
                for item in by[dy]:
                    action(remote(*item))
            if dy == 0:
                run()
            elif dy * sign == 1:
                pl.when(gy < ny - 1)(run)
            else:
                pl.when(gy > 0)(run)

    def start(by):
        each(by, lambda c: c.start(), 1)

    def wait_beside(by):
        each(by, lambda c: c.wait_recv(), -1, (0,))

    def wait_halo(by):
        each(by, lambda c: c.wait_recv(), -1, (1, -1))

    def wait_send(by):
        each(by, lambda c: c.wait_send(), 1)

    def half_entries(b):
        fs = pl.ds(b * HALF, HALF)
        ft = pl.ds(b * HALF, THIRD[b])
        return [
            (0, 1, rows.at[pl.ds(9, 2), fs], rows.at[pl.ds(1, 2), fs]),
            (0, 1, rows.at[pl.ds(8, 1), ft], rows.at[pl.ds(0, 1), ft]),
            (0, -1, rows.at[pl.ds(3, 2), fs], rows.at[pl.ds(11, 2), fs]),
            (0, -1, rows.at[pl.ds(5, 1), ft], rows.at[pl.ds(13, 1), ft]),
            (1, 0, packed.at[b], beside.at[b, 0]),
            (-1, 0, packed.at[b], beside.at[b, 1]),
            (1, 1, packed.at[b, 3], corner.at[b, 0, 0]),
            (-1, 1, packed.at[b, 3], corner.at[b, 0, 1]),
            (1, -1, packed.at[b, 0], corner.at[b, 1, 0]),
            (-1, -1, packed.at[b, 0], corner.at[b, 1, 1]),
        ]

    half_a = group(half_entries(0), 0)
    half_b = group(half_entries(1), 10)
    half_r = group([
        (0, 1, rhs_rows.at[pl.ds(8, 3)], rhs_rows.at[pl.ds(0, 3)]),
        (0, -1, rhs_rows.at[pl.ds(3, 3)], rhs_rows.at[pl.ds(11, 3)]),
        (1, 0, rhs_packed, rhs_beside.at[0]),
        (-1, 0, rhs_packed, rhs_beside.at[1]),
        (1, 1, rhs_packed, rhs_corner.at[0, 0]),
        (-1, 1, rhs_packed, rhs_corner.at[0, 1]),
        (1, -1, rhs_packed, rhs_corner.at[1, 0]),
        (-1, -1, rhs_packed, rhs_corner.at[1, 1]),
    ], 20)

    for n in (0, 2, 3):
        loads[n].wait()
    load_half(0)
    pl.semaphore_wait(barrier, count - 1)
    straight = {1: half_a[1][:2], -1: half_a[-1][:2], 0: []}
    strips = {1: half_a[1][2:], -1: half_a[-1][2:], 0: half_a[0]}
    start(straight)
    pack_half(0)
    start(strips)
    for n in (1, 4, 5):
        loads[n].wait()
    load_half(1)
    pack_half(1)
    start(half_b)

    def wide(r, f):
        return jnp.concatenate([rows[r, f], edges[r, f]], axis=1)

    def upwind(fields, lo, hi, size, stride=None):
        def some(r0):
            span = range(size)
            for i in span:
                r = r0 + i
                cx, cz = wide(r, CX), wide(r, CZ)
                inv = 1.0 / wide(r, RHO)
                cx_p, cx_n = jnp.maximum(cx, 0.0), jnp.minimum(cx, 0.0)
                cz_p, cz_n = jnp.maximum(cz, 0.0), jnp.minimum(cz, 0.0)
                cy, cu = wide(r, CY), wide(r + 1, CY)
                cy_p, cy_n = jnp.maximum(cy, 0.0), jnp.minimum(cy, 0.0)
                cu_p, cu_n = jnp.maximum(cu, 0.0), jnp.minimum(cu, 0.0)
                for n, f in fields:
                    here = wide(r, f)
                    fx = cx_p * xm(here) + cx_n * here
                    fz = cz_p * zm(here) + cz_n * here
                    fy = cy_p * wide(r - 1, f) + cy_n * here
                    fu = cu_p * here + cu_n * wide(r + 1, f)
                    total = xp(fx) - fx + fu - fy + zp(fz) - fz
                    first[r, n] = here - total * inv
        grouped(lo, hi, size, some, stride)

    def face(c, a, b):
        return 0.5 * jnp.abs(c) - c * c / (a + b)

    def antidiffuse(fields, lo, hi, size, stride=None):
        def some(r0):
            ku = face(wide(r0, CY), wide(r0 - 1, RHO), wide(r0, RHO))
            for i in range(size):
                r = r0 + i
                rho = wide(r, RHO)
                inv = 1.0 / rho
                ky, ku = ku, face(wide(r + 1, CY), rho, wide(r + 1, RHO))
                kx = face(wide(r, CX), xm(rho), rho)
                kz = face(wide(r, CZ), zm(rho), rho)
                for n in fields:
                    here = first[r, n]
                    ax = kx * (here - xm(here))
                    az = kz * (here - zm(here))
                    ay = ky * (here - first[r - 1, n])
                    au = ku * (first[r + 1, n] - here)
                    total = xp(ax) - ax + au - ay + zp(az) - az
                    second[r, n] = here - total * inv
        grouped(lo, hi, size, some, stride)

    wind = ((0, U), (1, V), (2, W))
    wait_beside(half_a)
    unpack_own(0)
    upwind(wind, 4, 10, 3)
    antidiffuse((0, 1, 2), 5, 9, 2)
    wait_halo(half_a)
    unpack_halo(0)
    upwind(wind, 1, 19, 3, 9)
    antidiffuse((0, 1, 2), 2, 16, 3, 7)

    acc = jnp.zeros((nz, 128), jnp.float32)
    for j in range(ny_dev):
        r = 3 + j
        u, w = second[r, 0], second[r, 2]
        value = (0.5 * (xp(u) - xm(u)) + 0.5 * (second[r + 1, 1] - second[r - 1, 1])
                 + 0.5 * (zp(w) - zm(w)))[:, :128]
        rhs_rows[r] = value
        acc = jnp.where(slot == j, pltpu.roll(value, 8 * j + 4, 1), acc)
    rhs_packed[...] = acc
    start(half_r)

    wait_beside(half_b)
    unpack_own(1)
    wait_halo(half_b)
    unpack_halo(1)

    def make_coef(r0):
        size = 4
        a22s = [wide(r0 + i - 1, A22) for i in range(size + 2)]
        wys = []
        for i in range(size + 1):
            at = gy * ny_dev + r0 + i - 3
            wys.append(jnp.where((at > 0) & (at < ny * ny_dev), 0.5 * (a22s[i] + a22s[i + 1]), 0.0))
        for i in range(size):
            r = r0 + i
            a11, a33 = wide(r, A11), wide(r, A33)
            wxl = 0.5 * (xm(a11) + a11)
            wx = xp(wxl)
            wyl, wy = wys[i], wys[i + 1]
            wzl = jnp.where(ground, 0.0, 0.5 * (zm(a33) + a33))
            wz = zp(wzl)
            coef[r, 0] = wx
            coef[r, 1] = wxl
            coef[r, 2] = wy
            coef[r, 3] = wyl
            coef[r, 4] = wz
            coef[r, 5] = wzl
            coef[r, 6] = (SHIFT - HELM) - (wx + wxl + wy + wyl + wz + wzl)
            coef[r, 7] = 0.25 * wide(r, A12)
            coef[r, 8] = 0.25 * wide(r, A13)
            coef[r, 9] = 0.25 * wide(r, A23)

    grouped(1, 13, 4, make_coef)

    def spread_rhs(j, tile, row):
        edge = pltpu.roll(tile, 128 - (8 * j + 4), 1)
        kry[0, row] = jnp.concatenate([rhs_rows[row], edge], axis=1)

    def halo_rhs(side, js, lo, inside):
        @pl.when(inside)
        def _():
            tile = jnp.where(from_left, rhs_corner[side, 0], rhs_corner[side, 1])
            for n, j in enumerate(js):
                spread_rhs(j, tile, lo + n)

        @pl.when(jnp.logical_not(inside))
        def _():
            for n in range(3):
                kry[0, lo + n] = jnp.zeros((nz, 256), jnp.float32)

    def operate(n, r0, size):
        def sides(r):
            p = kry[n, r]
            right, left = xp(p), xm(p)
            return right, left, right - left

        here, above = sides(r0), sides(r0 + 1)
        below_dx = sides(r0 - 1)[2]
        out = []
        for i in range(size):
            r = r0 + i
            p, up, down = kry[n, r], kry[n, r + 1], kry[n, r - 1]
            if i > 0:
                below_dx, here, above = here[2], above, sides(r + 1)
            right, left, dx = here
            dy = up - down
            out.append(
                coef[r, 0] * right + coef[r, 1] * left + coef[r, 2] * up + coef[r, 3] * down
                + coef[r, 4] * zp(p) + coef[r, 5] * zm(p) + coef[r, 6] * p
                + coef[r, 7] * (above[2] - below_dx)
                + coef[r, 8] * (zp(dx) - zm(dx)) + coef[r, 9] * (zp(dy) - zm(dy)))
        return out

    def lift(n, lo, hi, size, stride=None):
        def some(r0):
            for i, value in enumerate(operate(n, r0, size)):
                kry[n + 1, r0 + i] = value
        grouped(lo, hi, size, some, stride)

    pairs = [(a, b) for a in range(ITERS + 1) for b in range(a, ITERS + 1)]

    def gram(acc, r0, size):
        tops = operate(ITERS - 1, r0, size)
        acc = list(acc)
        for i in range(size):
            vecs = [kry[n, r0 + i][:, :128] for n in range(ITERS)] + [tops[i][:, :128]]
            for n, (a, b) in enumerate(pairs):
                prod = vecs[a] * vecs[b]
                acc[n] = acc[n] + (prod[:8] + prod[8:])
        return tuple(acc)

    wait_beside(half_r)
    tile = jnp.where(from_left, rhs_beside[0], rhs_beside[1])
    for j in range(ny_dev):
        spread_rhs(j, tile, 3 + j)
    lift(0, 4, 10, 3)
    lift(1, 5, 9, 4)
    sums = gram(tuple(jnp.zeros((8, 128), jnp.float32) for _ in pairs), 6, 2)
    wait_halo(half_r)
    halo_rhs(0, (5, 6, 7), 0, gy > 0)
    halo_rhs(1, (0, 1, 2), 11, gy < ny - 1)
    lift(0, 1, 19, 3, 9)
    lift(1, 2, 16, 3, 7)
    sums = gram(gram(sums, 3, 3), 8, 3)
    spot = lax.broadcasted_iota(jnp.int32, (16, 128), 0)
    tile = jnp.zeros((16, 128), jnp.float32)
    for n, s in enumerate(sums):
        tile = jnp.where(spot == n, jnp.sum(s, axis=0, keepdims=True), tile)
    half = lane < 64
    folded = tile + pltpu.roll(tile, 64, 1)
    part[...] = jnp.where(half[:8], folded[:8], folded[8:])

    def part_copy(d):
        return pltpu.make_async_remote_copy(
            src_ref=part, dst_ref=parts.at[d - 1], send_sem=send_sem.at[27 + d],
            recv_sem=recv_sem.at[27 + d], device_id=peer(d), device_id_type=MESH)

    every_peer(lambda d: part_copy(d).start())
    upwind(((3, TH),), 2, 12, 5)
    antidiffuse((3,), 3, 11, 4)

    def store(ref, base, j, value):
        ref[pl.ds(base + j, nz, stride=ny_dev), :] = value

    for j in range(ny_dev):
        store(th_out, 0, j, second[3 + j, 3][:, :128])
    every_peer(lambda d: part_copy(d).wait_recv())
    if count <= 64:
        tile = part[...]
        for d in range(1, count):
            tile = tile + parts[d - 1]
    else:
        tile = lax.fori_loop(1, count, lambda d, acc: acc + parts[d - 1], part[...])
    low = jnp.sum(jnp.where(half[:8], tile, 0.0), axis=1, keepdims=True)
    high = jnp.sum(jnp.where(half[:8], 0.0, tile), axis=1, keepdims=True)
    gmat = {}
    for n, (a, b) in enumerate(pairs):
        gmat[a, b] = gmat[b, a] = low[n:n + 1, :] if n < 8 else high[n - 8:n - 7, :]

    def dot(a, b):
        terms = [x * y for x, y in zip(a, b) if x is not None and y is not None]
        return functools.reduce(lambda s, t: s + t, terms)

    def minus(a, s, b):
        out = []
        for x, y in zip(a, b):
            if y is None:
                out.append(x)
            else:
                out.append(-(s * y) if x is None else x - s * y)
        return out

    def image(a):
        out = [None if x is None else -SHIFT * x for x in a]
        for n in range(ITERS):
            if a[n] is not None:
                out[n + 1] = a[n] if out[n + 1] is None else out[n + 1] + a[n]
        return out

    one = jnp.ones((1, 1), jnp.float32)
    resid = [one] + [None] * ITERS
    dirs, images, duals, norms = [resid], [image(resid)], [], []
    press = [None] * (ITERS + 1)
    for step in range(ITERS):
        q = images[step]
        dual = [dot([gmat[a, b] for b in range(ITERS + 1)], q) for a in range(ITERS + 1)]
        duals.append(dual)
        norms.append(dot(q, dual))
        beta = dot(resid, dual) / norms[step]
        press = minus(press, -beta, dirs[step])
        if step + 1 < ITERS:
            resid = minus(resid, beta, q)
            lifted = image(resid)
            new_dir, new_img = resid, lifted
            for back in range(step + 1):
                alpha = dot(lifted, duals[back]) / norms[back]
                new_dir = minus(new_dir, alpha, dirs[back])
                new_img = minus(new_img, alpha, images[back])
            dirs.append(new_dir)
            images.append(new_img)
    c0, c1, c2 = [jnp.broadcast_to(c, (nz, 256)) for c in press[:ITERS]]

    def pressure(r):
        return c0 * kry[0, r] + c1 * kry[1, r] + c2 * kry[2, r]

    def finish(j0):
        size = 4
        ps = [pressure(3 + j0 + i - 1) for i in range(size + 2)]
        for i in range(size):
            j = j0 + i
            r = 3 + j
            down, here, up = ps[i:i + 3]
            store(p_out, 0, j, here[:, :128])
            store(mom_out, 0, j, (second[r, 0] - 0.5 * (xp(here) - xm(here)))[:, :128])
            store(mom_out, plane, j, (second[r, 1] - 0.5 * (up - down))[:, :128])
            store(mom_out, 2 * plane, j, (second[r, 2] - 0.5 * (zp(here) - zm(here)))[:, :128])

    grouped(0, ny_dev, 4, finish)

    wait_send(half_a)
    wait_send(half_b)
    wait_send(half_r)
    every_peer(lambda d: part_copy(d).wait_send())


def solution(mesh):
    nx, ny = mesh.shape["gx"], mesh.shape["gy"]

    def local(momenta, theta, courant, density, metric_diag, metric_cross):
        nz, ny_dev, nx_dev = density.shape
        args = (momenta, theta, courant, density, metric_diag, metric_cross)
        flat = [pltpu.with_memory_space_constraint(a.reshape(-1, nx_dev), pltpu.HBM) for a in args]
        plane = nz * ny_dev
        f32 = jnp.float32
        n_ext = ny_dev + 6
        n_sem = 28 + nx * ny - 1
        shape = jax.ShapeDtypeStruct
        vmem = pltpu.VMEM
        mom, th, press = pl.pallas_call(
            functools.partial(kernel, nx, ny),
            out_shape=(shape((3 * plane, nx_dev), f32), shape((plane, nx_dev), f32),
                       shape((plane, nx_dev), f32)),
            in_specs=[pl.BlockSpec(memory_space=pltpu.HBM)] * 6,
            out_specs=[pl.BlockSpec(memory_space=pltpu.VMEM)] * 3,
            scratch_shapes=[
                vmem((14 * plane, nx_dev), f32),
                vmem((n_ext, 14, nz, nx_dev), f32),
                vmem((n_ext, 14, nz, nx_dev), f32),
                vmem((2, 4, nz, nx_dev), f32),
                vmem((2, 2, 4, nz, nx_dev), f32),
                vmem((2, 2, 2, nz, nx_dev), f32),
                vmem((n_ext, 4, nz, 2 * nx_dev), f32),
                vmem((n_ext, 4, nz, 2 * nx_dev), f32),
                vmem((n_ext, 10, nz, 2 * nx_dev), f32),
                vmem((3, n_ext, nz, 2 * nx_dev), f32),
                vmem((n_ext, nz, nx_dev), f32),
                vmem((nz, nx_dev), f32),
                vmem((2, nz, nx_dev), f32),
                vmem((2, 2, nz, nx_dev), f32),
                vmem((8, 128), f32),
                vmem((nx * ny - 1, 8, 128), f32),
                pltpu.SemaphoreType.DMA((6,)),
                pltpu.SemaphoreType.DMA((n_sem,)),
                pltpu.SemaphoreType.DMA((n_sem,)),
            ],
            compiler_params=pltpu.CompilerParams(
                collective_id=0, has_side_effects=True, vmem_limit_bytes=40 * 1024 * 1024),
        )(*flat)
        return mom.reshape(momenta.shape), th.reshape(theta.shape), press.reshape(theta.shape)

    placed = (
        P(None, None, "gy", "gx"),
        P(None, "gy", "gx"),
        P(None, None, "gy", "gx"),
        P(None, "gy", "gx"),
        P(None, None, "gy", "gx"),
        P(None, None, "gy", "gx"),
    )
    return jax.shard_map(
        local,
        mesh=mesh,
        in_specs=placed,
        out_specs=(P(None, None, "gy", "gx"), P(None, "gy", "gx"), P(None, "gy", "gx")),
        check_vma=False,
    )
```

```python
import functools

import jax
import jax.numpy as jnp
from jax import lax
from jax.experimental import pallas as pl
from jax.experimental.pallas import tpu as pltpu
from jax.sharding import PartitionSpec as P

ITERS = 3
HELM = 0.02
SHIFT = 6.0
MESH = pl.DeviceIdType.MESH

ORDER = (1, 5, 7, 0, 2, 4, 6, 9, 8, 10, 11, 12, 13, 3)
V, CY, RHO, U, W, CX, CZ, A22, A11, A33, A12, A13, A23, TH = range(14)
HALF = 7
THIRD = (2, 1)


def kernel(nx, ny, mom, theta, cour, dens, diag, cross, mom_out, th_out, p_out,
           cells, rows, edges, packed, beside, corner, first, second, coef,
           kry, rhs_rows, rhs_packed, rhs_beside, rhs_corner,
           part, parts, in_sem, send_sem, recv_sem):
    gx = lax.axis_index("gx")
    gy = lax.axis_index("gy")
    nz = rows.shape[2]
    ny_dev = 8
    plane = nz * ny_dev

    def device(dx, dy):
        return {"gx": lax.rem(gx + dx + nx, nx), "gy": gy + dy}

    barrier = pltpu.get_barrier_semaphore()
    count = nx * ny
    me = gx * ny + gy

    def peer(d):
        other = lax.rem(me + d, count)
        return {"gx": other // ny, "gy": lax.rem(other, ny)}

    def every_peer(body):
        if count <= 64:
            for d in range(1, count):
                body(d)
        else:
            def step(d, _):
                body(d)
                return 0
            lax.fori_loop(1, count, step, 0)

    every_peer(lambda d: pl.semaphore_signal(barrier, inc=1, device_id=peer(d), device_id_type=MESH))

    loads = []
    place = 0
    for n, ref in enumerate((mom, theta, cour, dens, diag, cross)):
        size = ref.shape[0]
        loads.append(pltpu.make_async_copy(ref, cells.at[pl.ds(place, size)], in_sem.at[n]))
        place += size
    for n in (0, 2, 3, 1, 4, 5):
        loads[n].start()

    def clear(lo):
        rows[lo:lo + 3] = jnp.zeros((3,) + rows.shape[1:], jnp.float32)
        edges[lo:lo + 3] = jnp.zeros((3,) + edges.shape[1:], jnp.float32)
        for i in range(lo, lo + 3):
            rows[i, RHO] = jnp.ones(rows.shape[2:], jnp.float32)
            edges[i, RHO] = jnp.ones(rows.shape[2:], jnp.float32)
        rhs_rows[lo:lo + 3] = jnp.zeros((3,) + rhs_rows.shape[1:], jnp.float32)

    pl.when(gy == 0)(lambda: clear(0))
    pl.when(gy == ny - 1)(lambda: clear(11))

    lane = lax.broadcasted_iota(jnp.int32, (nz, 128), 1)
    level = lax.broadcasted_iota(jnp.int32, (nz, 128), 0)
    slot = lane // 8
    from_left = lax.rem(lane, 8) < 4
    wide_level = lax.broadcasted_iota(jnp.int32, (nz, 256), 0)
    last = wide_level == nz - 1
    ground = wide_level == 0

    def xm(a):
        return pltpu.roll(a, 1, 1)

    def xp(a):
        return pltpu.roll(a, 255, 1)

    def zp(a):
        return jnp.where(last, 0.0, pltpu.roll(a, nz - 1, 0))

    def zm(a):
        return jnp.where(ground, 0.0, pltpu.roll(a, 1, 0))

    def grouped(lo, hi, size, body, stride=None):
        stride = size if stride is None else stride
        for r0 in range(lo, lo + (hi - lo) // stride * stride, stride):
            body(r0)

    def load_half(b):
        def some(j0):
            for j in (j0, j0 + 1):
                for f in range(b * HALF, b * HALF + HALF):
                    value = cells[pl.ds(ORDER[f] * plane + j, nz, stride=ny_dev), :]
                    if f == CY:
                        value = jnp.where(gy * ny_dev + j == 0, 0.0, value)
                    if f == CZ:
                        value = jnp.where(level == 0, 0.0, value)
                    rows[3 + j, f] = value
        grouped(0, ny_dev, 2, some)

    def pack_half(b):
        for t in range(ny_dev // 2):
            acc = jnp.zeros((nz, 128), jnp.float32)
            for side in range(2):
                for fi in range(HALF):
                    p = 64 * side + 8 * fi
                    moved = pltpu.roll(rows[3 + 2 * t + side, b * HALF + fi], (p + 4) % 128, 1)
                    acc = jnp.where(slot == p // 8, moved, acc)
            for fi in range(THIRD[b]):
                p = 56 + 64 * fi
                moved = pltpu.roll(rows[5 + 3 * (t // 2), b * HALF + fi], (p + 4) % 128, 1)
                acc = jnp.where(slot == p // 8, moved, acc)
            packed[b, t] = acc

    def spread(b, tile, side, row):
        for fi in range(HALF):
            p = 64 * side + 8 * fi
            edges[row, b * HALF + fi] = pltpu.roll(tile, (128 - (p + 4)) % 128, 1)

    def unpack_own(b):
        for t in range(ny_dev // 2):
            tile = jnp.where(from_left, beside[b, 0, t], beside[b, 1, t])
            for side in range(2):
                spread(b, tile, side, 3 + 2 * t + side)

    def unpack_halo(b):
        def one(side, near, third):
            tile = jnp.where(from_left, corner[b, side, 0], corner[b, side, 1])
            spread(b, tile, 0, near)
            spread(b, tile, 1, near + 1)
            for fi in range(THIRD[b]):
                edges[third, b * HALF + fi] = pltpu.roll(tile, (128 - (60 + 64 * fi)) % 128, 1)

        pl.when(gy > 0)(lambda: one(0, 1, 0))
        pl.when(gy < ny - 1)(lambda: one(1, 11, 13))

    def remote(src, dst, k, dx, dy):
        return pltpu.make_async_remote_copy(
            src_ref=src, dst_ref=dst, send_sem=send_sem.at[k], recv_sem=recv_sem.at[k],
            device_id=device(dx, dy), device_id_type=MESH)

    def group(entries, base):
        by = {1: [], -1: [], 0: []}
        for n, (dx, dy, src, dst) in enumerate(entries):
            by[dy].append((src, dst, base + n, dx, dy))
        return by

    def each(by, action, sign, order=(0, 1, -1)):
        for dy in order:
            def run(dy=dy):
                for item in by[dy]:
                    action(remote(*item))
            if dy == 0:
                run()
            elif dy * sign == 1:
                pl.when(gy < ny - 1)(run)
            else:
                pl.when(gy > 0)(run)

    def start(by):
        each(by, lambda c: c.start(), 1)

    def wait_beside(by):
        each(by, lambda c: c.wait_recv(), -1, (0,))

    def wait_halo(by):
        each(by, lambda c: c.wait_recv(), -1, (1, -1))

    def wait_send(by):
        each(by, lambda c: c.wait_send(), 1)

    def half_entries(b):
        fs = pl.ds(b * HALF, HALF - b)
        ft = pl.ds(b * HALF, THIRD[b])
        return [
            (0, 1, rows.at[pl.ds(9, 2), fs], rows.at[pl.ds(1, 2), fs]),
            (0, 1, rows.at[pl.ds(8, 1), ft], rows.at[pl.ds(0, 1), ft]),
            (0, -1, rows.at[pl.ds(3, 2), fs], rows.at[pl.ds(11, 2), fs]),
            (0, -1, rows.at[pl.ds(5, 1), ft], rows.at[pl.ds(13, 1), ft]),
            (1, 0, packed.at[b], beside.at[b, 0]),
            (-1, 0, packed.at[b], beside.at[b, 1]),
            (1, 1, packed.at[b, 3], corner.at[b, 0, 0]),
            (-1, 1, packed.at[b, 3], corner.at[b, 0, 1]),
            (1, -1, packed.at[b, 0], corner.at[b, 1, 0]),
            (-1, -1, packed.at[b, 0], corner.at[b, 1, 1]),
        ]

    half_a = group(half_entries(0), 0)
    half_b = group(half_entries(1), 10)
    theta = pl.ds(TH, 1)
    half_t = group([
        (0, 1, rows.at[pl.ds(9, 2), theta], rows.at[pl.ds(1, 2), theta]),
        (0, -1, rows.at[pl.ds(3, 2), theta], rows.at[pl.ds(11, 2), theta]),
    ], 27 + count)
    half_r = group([
        (0, 1, rhs_rows.at[pl.ds(8, 3)], rhs_rows.at[pl.ds(0, 3)]),
        (0, -1, rhs_rows.at[pl.ds(3, 3)], rhs_rows.at[pl.ds(11, 3)]),
        (1, 0, rhs_packed, rhs_beside.at[0]),
        (-1, 0, rhs_packed, rhs_beside.at[1]),
        (1, 1, rhs_packed, rhs_corner.at[0, 0]),
        (-1, 1, rhs_packed, rhs_corner.at[0, 1]),
        (1, -1, rhs_packed, rhs_corner.at[1, 0]),
        (-1, -1, rhs_packed, rhs_corner.at[1, 1]),
    ], 20)

    for n in (0, 2, 3):
        loads[n].wait()
    load_half(0)
    pl.semaphore_wait(barrier, count - 1)
    straight = {1: half_a[1][:2], -1: half_a[-1][:2], 0: []}
    strips = {1: half_a[1][2:], -1: half_a[-1][2:], 0: half_a[0]}
    start(straight)
    pack_half(0)
    start(strips)
    for n in (1, 4, 5):
        loads[n].wait()
    load_half(1)
    pack_half(1)
    start(half_b)

    def wide(r, f):
        return jnp.concatenate([rows[r, f], edges[r, f]], axis=1)

    def upwind(fields, lo, hi, size, stride=None):
        def some(r0):
            span = range(size)
            for i in span:
                r = r0 + i
                cx, cz = wide(r, CX), wide(r, CZ)
                inv = 1.0 / wide(r, RHO)
                cx_p, cx_n = jnp.maximum(cx, 0.0), jnp.minimum(cx, 0.0)
                cz_p, cz_n = jnp.maximum(cz, 0.0), jnp.minimum(cz, 0.0)
                cy, cu = wide(r, CY), wide(r + 1, CY)
                cy_p, cy_n = jnp.maximum(cy, 0.0), jnp.minimum(cy, 0.0)
                cu_p, cu_n = jnp.maximum(cu, 0.0), jnp.minimum(cu, 0.0)
                for n, f in fields:
                    here = wide(r, f)
                    fx = cx_p * xm(here) + cx_n * here
                    fz = cz_p * zm(here) + cz_n * here
                    fy = cy_p * wide(r - 1, f) + cy_n * here
                    fu = cu_p * here + cu_n * wide(r + 1, f)
                    total = xp(fx) - fx + fu - fy + zp(fz) - fz
                    first[r, n] = here - total * inv
        grouped(lo, hi, size, some, stride)

    def face(c, a, b):
        return 0.5 * jnp.abs(c) - c * c / (a + b)

    def antidiffuse(fields, lo, hi, size, stride=None):
        def some(r0):
            ku = face(wide(r0, CY), wide(r0 - 1, RHO), wide(r0, RHO))
            for i in range(size):
                r = r0 + i
                rho = wide(r, RHO)
                inv = 1.0 / rho
                ky, ku = ku, face(wide(r + 1, CY), rho, wide(r + 1, RHO))
                kx = face(wide(r, CX), xm(rho), rho)
                kz = face(wide(r, CZ), zm(rho), rho)
                for n in fields:
                    here = first[r, n]
                    ax = kx * (here - xm(here))
                    az = kz * (here - zm(here))
                    ay = ky * (here - first[r - 1, n])
                    au = ku * (first[r + 1, n] - here)
                    total = xp(ax) - ax + au - ay + zp(az) - az
                    second[r, n] = here - total * inv
        grouped(lo, hi, size, some, stride)

    wind = ((0, U), (1, V), (2, W))
    wait_beside(half_a)
    unpack_own(0)
    upwind(wind, 4, 10, 3)
    antidiffuse((0, 1, 2), 5, 9, 2)
    wait_halo(half_a)
    unpack_halo(0)
    upwind(wind, 1, 19, 3, 9)
    antidiffuse((0, 1, 2), 2, 16, 3, 7)

    acc = jnp.zeros((nz, 128), jnp.float32)
    for j in range(ny_dev):
        r = 3 + j
        u, w = second[r, 0], second[r, 2]
        value = (0.5 * (xp(u) - xm(u)) + 0.5 * (second[r + 1, 1] - second[r - 1, 1])
                 + 0.5 * (zp(w) - zm(w)))[:, :128]
        rhs_rows[r] = value
        acc = jnp.where(slot == j, pltpu.roll(value, 8 * j + 4, 1), acc)
    rhs_packed[...] = acc
    start(half_r)
    start(half_t)

    wait_beside(half_b)
    unpack_own(1)
    wait_halo(half_b)
    unpack_halo(1)

    def make_coef(r0):
        size = 4
        a22s = [wide(r0 + i - 1, A22) for i in range(size + 2)]
        wys = []
        for i in range(size + 1):
            at = gy * ny_dev + r0 + i - 3
            wys.append(jnp.where((at > 0) & (at < ny * ny_dev), 0.5 * (a22s[i] + a22s[i + 1]), 0.0))
        for i in range(size):
            r = r0 + i
            a11, a33 = wide(r, A11), wide(r, A33)
            wxl = 0.5 * (xm(a11) + a11)
            wx = xp(wxl)
            wyl, wy = wys[i], wys[i + 1]
            wzl = jnp.where(ground, 0.0, 0.5 * (zm(a33) + a33))
            wz = zp(wzl)
            coef[r, 0] = wx
            coef[r, 1] = wxl
            coef[r, 2] = wy
            coef[r, 3] = wyl
            coef[r, 4] = wz
            coef[r, 5] = wzl
            coef[r, 6] = (SHIFT - HELM) - (wx + wxl + wy + wyl + wz + wzl)
            coef[r, 7] = 0.25 * wide(r, A12)
            coef[r, 8] = 0.25 * wide(r, A13)
            coef[r, 9] = 0.25 * wide(r, A23)

    grouped(1, 13, 4, make_coef)

    def spread_rhs(j, tile, row):
        edge = pltpu.roll(tile, 128 - (8 * j + 4), 1)
        kry[0, row] = jnp.concatenate([rhs_rows[row], edge], axis=1)

    def halo_rhs(side, js, lo, inside):
        @pl.when(inside)
        def _():
            tile = jnp.where(from_left, rhs_corner[side, 0], rhs_corner[side, 1])
            for n, j in enumerate(js):
                spread_rhs(j, tile, lo + n)

        @pl.when(jnp.logical_not(inside))
        def _():
            for n in range(3):
                kry[0, lo + n] = jnp.zeros((nz, 256), jnp.float32)

    def operate(n, r0, size):
        def sides(r):
            p = kry[n, r]
            right, left = xp(p), xm(p)
            return right, left, right - left

        here, above = sides(r0), sides(r0 + 1)
        below_dx = sides(r0 - 1)[2]
        out = []
        for i in range(size):
            r = r0 + i
            p, up, down = kry[n, r], kry[n, r + 1], kry[n, r - 1]
            if i > 0:
                below_dx, here, above = here[2], above, sides(r + 1)
            right, left, dx = here
            dy = up - down
            out.append(
                coef[r, 0] * right + coef[r, 1] * left + coef[r, 2] * up + coef[r, 3] * down
                + coef[r, 4] * zp(p) + coef[r, 5] * zm(p) + coef[r, 6] * p
                + coef[r, 7] * (above[2] - below_dx)
                + coef[r, 8] * (zp(dx) - zm(dx)) + coef[r, 9] * (zp(dy) - zm(dy)))
        return out

    def lift(n, lo, hi, size, stride=None):
        def some(r0):
            for i, value in enumerate(operate(n, r0, size)):
                kry[n + 1, r0 + i] = value
        grouped(lo, hi, size, some, stride)

    pairs = [(a, b) for a in range(ITERS + 1) for b in range(a, ITERS + 1)]

    def gram(acc, r0, size):
        tops = operate(ITERS - 1, r0, size)
        acc = list(acc)
        for i in range(size):
            vecs = [kry[n, r0 + i][:, :128] for n in range(ITERS)] + [tops[i][:, :128]]
            for n, (a, b) in enumerate(pairs):
                prod = vecs[a] * vecs[b]
                acc[n] = acc[n] + (prod[:8] + prod[8:])
        return tuple(acc)

    wait_beside(half_r)
    tile = jnp.where(from_left, rhs_beside[0], rhs_beside[1])
    for j in range(ny_dev):
        spread_rhs(j, tile, 3 + j)
    lift(0, 4, 10, 3)
    lift(1, 5, 9, 4)
    sums = gram(tuple(jnp.zeros((8, 128), jnp.float32) for _ in pairs), 6, 2)
    wait_halo(half_r)
    halo_rhs(0, (5, 6, 7), 0, gy > 0)
    halo_rhs(1, (0, 1, 2), 11, gy < ny - 1)
    lift(0, 1, 19, 3, 9)
    lift(1, 2, 16, 3, 7)
    sums = gram(gram(sums, 3, 3), 8, 3)
    spot = lax.broadcasted_iota(jnp.int32, (16, 128), 0)
    tile = jnp.zeros((16, 128), jnp.float32)
    for n, s in enumerate(sums):
        tile = jnp.where(spot == n, jnp.sum(s, axis=0, keepdims=True), tile)
    half = lane < 64
    folded = tile + pltpu.roll(tile, 64, 1)
    part[...] = jnp.where(half[:8], folded[:8], folded[8:])

    def part_copy(d):
        return pltpu.make_async_remote_copy(
            src_ref=part, dst_ref=parts.at[d - 1], send_sem=send_sem.at[27 + d],
            recv_sem=recv_sem.at[27 + d], device_id=peer(d), device_id_type=MESH)

    every_peer(lambda d: part_copy(d).start())
    wait_halo(half_t)
    upwind(((3, TH),), 2, 12, 5)
    antidiffuse((3,), 3, 11, 4)

    def store(ref, base, j, value):
        ref[pl.ds(base + j, nz, stride=ny_dev), :] = value

    for j in range(ny_dev):
        store(th_out, 0, j, second[3 + j, 3][:, :128])
    every_peer(lambda d: part_copy(d).wait_recv())
    if count <= 64:
        tile = part[...]
        for d in range(1, count):
            tile = tile + parts[d - 1]
    else:
        tile = lax.fori_loop(1, count, lambda d, acc: acc + parts[d - 1], part[...])
    low = jnp.sum(jnp.where(half[:8], tile, 0.0), axis=1, keepdims=True)
    high = jnp.sum(jnp.where(half[:8], 0.0, tile), axis=1, keepdims=True)
    gmat = {}
    for n, (a, b) in enumerate(pairs):
        gmat[a, b] = gmat[b, a] = low[n:n + 1, :] if n < 8 else high[n - 8:n - 7, :]

    def dot(a, b):
        terms = [x * y for x, y in zip(a, b) if x is not None and y is not None]
        return functools.reduce(lambda s, t: s + t, terms)

    def minus(a, s, b):
        out = []
        for x, y in zip(a, b):
            if y is None:
                out.append(x)
            else:
                out.append(-(s * y) if x is None else x - s * y)
        return out

    def image(a):
        out = [None if x is None else -SHIFT * x for x in a]
        for n in range(ITERS):
            if a[n] is not None:
                out[n + 1] = a[n] if out[n + 1] is None else out[n + 1] + a[n]
        return out

    one = jnp.ones((1, 1), jnp.float32)
    resid = [one] + [None] * ITERS
    dirs, images, duals, norms = [resid], [image(resid)], [], []
    press = [None] * (ITERS + 1)
    for step in range(ITERS):
        q = images[step]
        dual = [dot([gmat[a, b] for b in range(ITERS + 1)], q) for a in range(ITERS + 1)]
        duals.append(dual)
        norms.append(dot(q, dual))
        beta = dot(resid, dual) / norms[step]
        press = minus(press, -beta, dirs[step])
        if step + 1 < ITERS:
            resid = minus(resid, beta, q)
            lifted = image(resid)
            new_dir, new_img = resid, lifted
            for back in range(step + 1):
                alpha = dot(lifted, duals[back]) / norms[back]
                new_dir = minus(new_dir, alpha, dirs[back])
                new_img = minus(new_img, alpha, images[back])
            dirs.append(new_dir)
            images.append(new_img)
    c0, c1, c2 = [jnp.broadcast_to(c, (nz, 256)) for c in press[:ITERS]]

    def pressure(r):
        return c0 * kry[0, r] + c1 * kry[1, r] + c2 * kry[2, r]

    def finish(j0):
        size = 4
        ps = [pressure(3 + j0 + i - 1) for i in range(size + 2)]
        for i in range(size):
            j = j0 + i
            r = 3 + j
            down, here, up = ps[i:i + 3]
            store(p_out, 0, j, here[:, :128])
            store(mom_out, 0, j, (second[r, 0] - 0.5 * (xp(here) - xm(here)))[:, :128])
            store(mom_out, plane, j, (second[r, 1] - 0.5 * (up - down))[:, :128])
            store(mom_out, 2 * plane, j, (second[r, 2] - 0.5 * (zp(here) - zm(here)))[:, :128])

    grouped(0, ny_dev, 4, finish)

    wait_send(half_a)
    wait_send(half_b)
    wait_send(half_r)
    wait_send(half_t)
    every_peer(lambda d: part_copy(d).wait_send())


def solution(mesh):
    nx, ny = mesh.shape["gx"], mesh.shape["gy"]

    def local(momenta, theta, courant, density, metric_diag, metric_cross):
        nz, ny_dev, nx_dev = density.shape
        args = (momenta, theta, courant, density, metric_diag, metric_cross)
        flat = [pltpu.with_memory_space_constraint(a.reshape(-1, nx_dev), pltpu.HBM) for a in args]
        plane = nz * ny_dev
        f32 = jnp.float32
        n_ext = ny_dev + 6
        n_sem = 28 + nx * ny - 1 + 2
        shape = jax.ShapeDtypeStruct
        vmem = pltpu.VMEM
        mom, th, press = pl.pallas_call(
            functools.partial(kernel, nx, ny),
            out_shape=(shape((3 * plane, nx_dev), f32), shape((plane, nx_dev), f32),
                       shape((plane, nx_dev), f32)),
            in_specs=[pl.BlockSpec(memory_space=pltpu.HBM)] * 6,
            out_specs=[pl.BlockSpec(memory_space=pltpu.VMEM)] * 3,
            scratch_shapes=[
                vmem((14 * plane, nx_dev), f32),
                vmem((n_ext, 14, nz, nx_dev), f32),
                vmem((n_ext, 14, nz, nx_dev), f32),
                vmem((2, 4, nz, nx_dev), f32),
                vmem((2, 2, 4, nz, nx_dev), f32),
                vmem((2, 2, 2, nz, nx_dev), f32),
                vmem((n_ext, 4, nz, 2 * nx_dev), f32),
                vmem((n_ext, 4, nz, 2 * nx_dev), f32),
                vmem((n_ext, 10, nz, 2 * nx_dev), f32),
                vmem((3, n_ext, nz, 2 * nx_dev), f32),
                vmem((n_ext, nz, nx_dev), f32),
                vmem((nz, nx_dev), f32),
                vmem((2, nz, nx_dev), f32),
                vmem((2, 2, nz, nx_dev), f32),
                vmem((8, 128), f32),
                vmem((nx * ny - 1, 8, 128), f32),
                pltpu.SemaphoreType.DMA((6,)),
                pltpu.SemaphoreType.DMA((n_sem,)),
                pltpu.SemaphoreType.DMA((n_sem,)),
            ],
            compiler_params=pltpu.CompilerParams(
                collective_id=0, has_side_effects=True, vmem_limit_bytes=40 * 1024 * 1024),
        )(*flat)
        return mom.reshape(momenta.shape), th.reshape(theta.shape), press.reshape(theta.shape)

    placed = (
        P(None, None, "gy", "gx"),
        P(None, "gy", "gx"),
        P(None, None, "gy", "gx"),
        P(None, "gy", "gx"),
        P(None, None, "gy", "gx"),
        P(None, None, "gy", "gx"),
    )
    return jax.shard_map(
        local,
        mesh=mesh,
        in_specs=placed,
        out_specs=(P(None, None, "gy", "gx"), P(None, "gy", "gx"), P(None, "gy", "gx")),
        check_vma=False,
    )
```
